512 devices in a mesh: tm: 8 (over x, z_lo), row: 16 (over y, core), col: 4 (over z_hi).
Axes of the slice: x: 4, y: 8, z: 8 (z_hi: 4, z_lo: 2; z = z_hi * 2 + z_lo), core: 2. Of those that a mesh axis runs over, the one named last changes fastest.
Arguments:
- features: bfloat16 [16, 96, 128, 192], P('tm', 'row', 'col'), may hold values from -80 to 80
- cotangent: bfloat16 [16, 96, 128, 192], P('tm', 'row', 'col'), may hold values from -12 to 12
- kernel: bfloat16 [5184, 192], replicated, may hold values from -0.078125 to 0.078125
- gain: float32 [192], replicated, may hold values from 0.1 to 1.9
Outputs:
- feature_grad: bfloat16 [16, 96, 128, 192], P('tm', 'row', 'col')
- weight_grad: float32 [5184, 192], P(('row', 'col'))
- gain_grad: float32 [192], replicated
The draws below stay inside these ranges and needn't reach their ends.
All inputs are finite; a program needn't handle non-finite values.
Results may differ from the reference program's by a relative error of at most 0.0029.
Values may be sent and summed in bfloat16 or wider, within the bound.
A program may use at most 64 MiB of HBM per device.

```python
import math
import jax
import jax.numpy as jnp
from jax import lax

C = 192
FRAMES = 16
HEIGHT = 96
WIDTH = 128


def draw_features(key, part):
    key = jax.random.fold_in(key, 11)
    key_base, key_cell, key_chan = jax.random.split(key, 3)
    shape = (FRAMES, HEIGHT, WIDTH, C)
    cell_scale = jnp.exp(jax.random.uniform(key_cell, (FRAMES, HEIGHT, WIDTH, 1), jnp.float32, 0.0, math.log(10.0)))
    chan_scale = jnp.exp(jax.random.uniform(key_chan, (C,), jnp.float32, math.log(0.5), math.log(2.0)))
    base = jnp.clip(jax.random.normal(key_base, shape, jnp.float32), -4.0, 4.0)
    return (base * cell_scale * chan_scale).astype(jnp.bfloat16)


def draw_cotangent(key, part):
    key = jax.random.fold_in(key, 23)
    key_base = jax.random.fold_in(key, 0)
    shape = (FRAMES, HEIGHT, WIDTH, C)
    frame_pos = jnp.arange(FRAMES, dtype=jnp.float32).reshape(FRAMES, 1, 1, 1)
    ramp = 1.0 + 2.0 * frame_pos / (FRAMES - 1)
    base = jnp.clip(jax.random.normal(key_base, shape, jnp.float32), -4.0, 4.0)
    return (base * ramp).astype(jnp.bfloat16)


def normal_values(rng, extent, scale, reach, held_as=jnp.bfloat16):
    drawn = jax.random.normal(rng, extent, jnp.float32) * scale
    return jnp.minimum(jnp.maximum(drawn, -reach), reach).astype(held_as)


def setup_inputs(seed: int = 0) -> dict:
    seeds = jax.random.split(jax.random.key(seed), 5)
    features = draw_features(jax.random.fold_in(seeds[4], 71), 0)
    cotangent = draw_cotangent(jax.random.fold_in(seeds[4], 71), 0)
    kernel = normal_values(seeds[2], (27 * C, C), (27 * C) ** -0.5, 0.078125)
    gain = jnp.clip(1.0 + 0.18 * jax.random.normal(seeds[3], (C,), jnp.float32), 0.1, 1.9)
    return {"features": features, "cotangent": cotangent, "kernel": kernel, "gain": gain}


def reference(features, cotangent, kernel, gain):
    frames, height, width, chan = features.shape
    wide = features.astype(jnp.float32)
    inverse = lax.rsqrt(lax.optimization_barrier(jnp.mean(wide * wide, axis=-1, keepdims=True)) + 1e-06)
    normed = wide * inverse
    pre = normed * gain
    act = jax.nn.silu(pre).astype(jnp.bfloat16)
    act_pad = jnp.pad(act, ((2, 0), (1, 1), (1, 1), (0, 0)))
    grad_pad = jnp.pad(cotangent, ((0, 2), (1, 1), (1, 1), (0, 0)))
    grad_rows = cotangent.reshape(-1, chan)
    scale = 1.0 / math.sqrt(frames * height * width)
    pieces = []
    back = jnp.zeros((frames * height * width, chan), jnp.float32)
    for shift_t in range(3):
        for shift_r in range(3):
            for shift_c in range(3):
                tap = (shift_t * 3 + shift_r) * 3 + shift_c
                weights = kernel[tap * chan:(tap + 1) * chan]
                act_rows = act_pad[shift_t:shift_t + frames, shift_r:shift_r + height, shift_c:shift_c + width].reshape(-1, chan)
                pieces.append(jnp.dot(act_rows.T, grad_rows, preferred_element_type=jnp.float32))
                grad_slice = grad_pad[2 - shift_t:2 - shift_t + frames, 2 - shift_r:2 - shift_r + height, 2 - shift_c:2 - shift_c + width].reshape(-1, chan)
                back = back + jnp.dot(grad_slice, weights.T, preferred_element_type=jnp.float32)
    weight_grad = jnp.concatenate(pieces, axis=0) * scale
    dact = back.reshape(features.shape)
    sigma = jax.nn.sigmoid(pre)
    dpre = dact * sigma * (1.0 + pre * (1.0 - sigma))
    gain_grad = lax.optimization_barrier(jnp.sum(dpre * normed, axis=(0, 1, 2))) * scale
    dnormed = dpre * gain
    project = lax.optimization_barrier(jnp.mean(dnormed * normed, axis=-1, keepdims=True))
    feature_grad = (cotangent.astype(jnp.float32) + inverse * (dnormed - normed * project)).astype(jnp.bfloat16)
    return (feature_grad, weight_grad, gain_grad)
```

```python
import math

import jax
import jax.numpy as jnp
from jax import lax
from jax.experimental import pallas as pl
from jax.experimental.pallas import tpu as pltpu
from jax.sharding import PartitionSpec as P

MESH = pl.DeviceIdType.MESH
F32 = jnp.float32
BF16 = jnp.bfloat16
C = 192
ROWS, COLS = 6, 32
CELLS = 2 * ROWS * COLS
PIECES = 4
HALF_TAPS = 14
WIN = 144

HALO = [(-1, 0, 0)]
HALO += [(dt, dr, 0) for dt in (0, -1) for dr in (-1, 1)]
HALO += [(dt, dr, dc) for dt in (0, -1) for dc in (-1, 1) for dr in (-1, 0, 1)]


def body(
    feat, cot, w_hbm, gain, fg_out, wg_out, gg_out,
    w_v, big, cols, act_t, packs, rows16, act32, dact_v, wgl, xsend, xrecv,
    gpart, grecv, ysend, yrecv, zsend, zrecv, bsend, brecv, fin,
    w_sem, halo_s, halo_r, pair_s, pair_r, x_s, x_r, g_s, g_r, y_s, y_r, z_s, z_r, b_s, b_r,
):
    tm, row, col = lax.axis_index("tm"), lax.axis_index("row"), lax.axis_index("col")
    x, zlo = tm // 2, tm % 2
    y, core = row // 2, row % 2
    z = col * 2 + zlo
    other = 1 - core
    self_y = core == y // 4
    self_b = x == col

    def near(dt, dr, dc):
        return ((tm + dt + 8) % 8, (row + dr + 16) % 16, (col + dc + 4) % 4)

    partner = (tm, 2 * y + other, col)

    def x_dev(step):
        return (((x + step) % 4) * 2 + zlo, row, col)

    def remote(src, dst, send, recv, device):
        return pltpu.make_async_remote_copy(
            src_ref=src, dst_ref=dst, send_sem=send, recv_sem=recv, device_id=device, device_id_type=MESH
        )

    weights = pltpu.make_async_copy(w_hbm, w_v, w_sem)
    weights.start()

    barrier = pltpu.get_barrier_semaphore()

    def greet(device):
        pl.semaphore_signal(barrier, inc=1, device_id=device, device_id_type=MESH)

    for dt, dr, dc in HALO:
        greet(near(-dt, -dr, -dc))
    greet(partner)
    for step in (1, 2, 3):
        greet(x_dev(-step + 4))
    for k in range(8):
        @pl.when(jnp.logical_not(jnp.logical_and(self_y, y == k)))
        def _():
            greet((tm, 2 * k + y // 4, col))

        @pl.when(z != k)
        def _():
            greet((2 * x + k % 2, row, k // 2))

        @pl.when(jnp.logical_not(jnp.logical_and(self_b, z == k)))
        def _():
            greet((2 * col + k % 2, row, k // 2))

    for side, q in ((0, 0), (1, COLS - 1)):
        rows16[side] = jnp.zeros((16, C), F32)
        for f in range(2):
            for r in range(ROWS):
                i = f * ROWS + r
                rows16[side, i : i + 1, :] = cot[f, r].astype(F32)[q : q + 1, :]
        packs[side] = rows16[side].astype(BF16)

    expected = 17 + 1 + 3 + 7 + 16
    pl.semaphore_wait(barrier, expected - self_y.astype(jnp.int32) - self_b.astype(jnp.int32))

    main = big.at[0, 1]
    halo = []
    for m, (dt, dr, dc) in enumerate(HALO):
        df = -dt
        if dc != 0:
            src = packs.at[0 if dc < 0 else 1]
            dst = cols.at[0, 1 if dc < 0 else 0, df, 1 - dr]
        elif dr == -1:
            src, dst = cot.at[:, 0], main.at[2 * df : 2 * df + 2, ROWS + 1]
        elif dr == 1:
            src, dst = cot.at[:, ROWS - 1], main.at[2 * df : 2 * df + 2, 0]
        else:
            src, dst = cot, main.at[2:4, 1 : ROWS + 1]
        halo.append(remote(src, dst, halo_s.at[m], halo_r.at[m], near(dt, dr, dc)))
        halo[-1].start()
    main[0:2, 1 : ROWS + 1] = cot[...]

    def norm():
        wide = feat[...].astype(F32).reshape(CELLS, C)
        inverse = lax.rsqrt(jnp.mean(wide * wide, axis=-1, keepdims=True) + 1e-06)
        normed = wide * inverse
        return inverse, normed, normed * gain[...]

    pre = norm()[2]
    act32[:, C:] = jnp.zeros((CELLS, 256 - C), F32)
    act32[:, :C] = pre * jax.nn.sigmoid(pre)
    act_t[0] = act32[...].T[:C].astype(BF16)
    swap = [remote(act_t.at[0], act_t.at[1], pair_s.at[0], pair_r.at[0], partner)]
    swap[0].start()

    for copy in halo:
        copy.wait_recv()

    @pl.when(row == 0)
    def _():
        main[:, 0] = jnp.zeros((4, COLS, C), BF16)
        cols[0, :, :, 0] = jnp.zeros((2, 2, 16, C), BF16)

    @pl.when(row == 15)
    def _():
        main[:, ROWS + 1] = jnp.zeros((4, COLS, C), BF16)
        cols[0, :, :, 2] = jnp.zeros((2, 2, 16, C), BF16)

    @pl.when(tm == 7)
    def _():
        main[2:4] = jnp.zeros((2, ROWS + 2, COLS, C), BF16)
        cols[0, :, 1] = jnp.zeros((2, 3, 16, C), BF16)

    @pl.when(col == 0)
    def _():
        cols[0, 0] = jnp.zeros((2, 3, 16, C), BF16)

    @pl.when(col == 3)
    def _():
        cols[0, 1] = jnp.zeros((2, 3, 16, C), BF16)

    swap.append(remote(main, big.at[1, 1], pair_s.at[1], pair_r.at[1], partner))
    swap.append(remote(cols.at[0], cols.at[1], pair_s.at[2], pair_r.at[2], partner))
    swap[1].start()
    swap[2].start()

    spot = lax.broadcasted_iota(jnp.int32, (COLS, C), 0)

    def shift(tile):
        for f in range(4):
            edges = [[cols[tile, s, f // 2, k].astype(F32) for k in range(3)] for s in (0, 1)]
            for r in range(ROWS + 2):
                k = 0 if r == 0 else 2 if r == ROWS + 1 else 1
                i = (f % 2) * ROWS + (r - 1) % ROWS
                value = big[tile, 1, f, r].astype(F32)
                after = jnp.where(spot == COLS - 1, edges[1][k][i : i + 1], pltpu.roll(value, COLS - 1, 0))
                before = jnp.where(spot == 0, edges[0][k][i : i + 1], pltpu.roll(value, 1, 0))
                big[tile, 0, f, r] = after.astype(BF16)
                big[tile, 2, f, r] = before.astype(BF16)

    shift(0)
    for copy in swap:
        copy.wait_recv()
    shift(1)

    lane = lax.broadcasted_iota(jnp.int32, (48, 128), 1)

    def pack(j):
        start = 96 + 80 * j + 16 * (j // 16)
        at = (j // 4) * WIN
        xsend[j % 4, at : at + 96] = wgl[start : start + 96, 0:128].astype(BF16)
        low = wgl[start : start + 48, 128:256]
        high = pltpu.roll(wgl[start + 48 : start + 96, 128:256], 64, 1)
        xsend[j % 4, at + 96 : at + WIN] = jnp.where(lane < 64, low, high).astype(BF16)

    span = 8 // PIECES * WIN
    sent = []

    def x_copy(p, step):
        part = slice(p * span, (p + 1) * span)
        return remote(
            xsend.at[(x + step) % 4, part], xrecv.at[step - 1, part],
            x_s.at[p, step - 1], x_r.at[p, step - 1], x_dev(step),
        )

    ready = 0
    for i in range(HALF_TAPS):
        tap = i + 13 * core
        a, b, c = tap // 9, (tap // 3) % 3, tap % 3
        total = jnp.zeros((C, C), F32)
        for tile in (0, 1):
            patch = big[tile, c, pl.ds(2 - a, 2), pl.ds(2 - b, ROWS)].reshape(CELLS, C)
            total += jnp.dot(act_t[tile], patch, preferred_element_type=F32)
        wgl[pl.ds(pl.multiple_of(i * C + 96 * other, 8), C), 0:C] = total
        while ready < 32 and C * (i + 1) >= C + 80 * ready + 16 * (ready // 16):
            pack(ready)
            ready += 1
            if ready % (32 // PIECES) == 0:
                for step in (1, 2, 3):
                    sent.append(x_copy(ready // (32 // PIECES) - 1, step))
                    sent[-1].start()

    weights.wait()
    dact = jnp.zeros((CELLS, C), F32)
    for tap in range(27):
        a, b, c = tap // 9, (tap // 3) % 3, tap % 3
        patch = big[0, c, 2 - a : 4 - a, 2 - b : 2 - b + ROWS].reshape(CELLS, C)
        dact += lax.dot_general(
            patch, w_v[tap * C : (tap + 1) * C], (((1,), (1,)), ((), ())), preferred_element_type=F32
        )
    inverse, normed, pre = norm()
    sigma = jax.nn.sigmoid(pre)
    dpre = dact * sigma * (1.0 + pre * (1.0 - sigma))
    gain_part = jnp.sum(dpre * normed, axis=0, keepdims=True)
    dnormed = dpre * gain[...]
    project = jnp.mean(dnormed * normed, axis=-1, keepdims=True)
    grad = cot[...].astype(F32).reshape(CELLS, C) + inverse * (dnormed - normed * project)
    fg_out[...] = grad.astype(BF16).reshape(2, ROWS, COLS, C)

    act32[0:1, C:] = jnp.zeros((1, 256 - C), F32)
    act32[0:1, :C] = gain_part
    gpart[...] = jnp.zeros((2, 8, 128), F32)
    gpart[0, 0:1] = act32[0:1, 0:128]
    gpart[0, 1:2] = act32[0:1, 128:256]
    pair_gain = remote(gpart.at[0], grecv.at[0], g_s.at[0], g_r.at[0], partner)
    pair_gain.start()
    pair_gain.wait()
    gpart[1] = gpart[0] + grecv[0]
    gain_copies = []
    for step in (1, 2, 3):
        gain_copies.append(remote(gpart.at[1], grecv.at[step], g_s.at[step], g_r.at[step], x_dev(step)))
        gain_copies[-1].start()
    for copy in gain_copies:
        copy.wait()
    gsum = gpart[1] + grecv[1] + grecv[2] + grecv[3]
    upper = gsum.astype(BF16)
    lower = (gsum - upper.astype(F32)).astype(BF16)
    gain_rows = jnp.concatenate([upper.astype(F32), lower.astype(F32)], axis=0).astype(BF16)

    def y_self(k):
        return jnp.logical_and(self_y, y == k)

    def y_copy(k):
        return remote(ysend.at[k], yrecv.at[y], y_s.at[k], y_r.at[y], (tm, 8 * core + k, col))

    for p in range(PIECES):
        for step in (1, 2, 3):
            x_copy(p, step).wait_recv()
        part = slice(p * span, (p + 1) * span)
        value = xsend[x, part].astype(F32)
        for step in (1, 2, 3):
            value += xrecv[step - 1, part].astype(F32)
        value = value.astype(BF16)
        for k in range(p * 8 // PIECES, (p + 1) * 8 // PIECES):
            at = k * WIN - p * span
            ysend[k, 0:WIN] = value[at : at + WIN]
            ysend[k, WIN : WIN + 16] = gain_rows
            mine = row == 8 * core + k

            @pl.when(jnp.logical_not(mine))
            def _():
                y_copy(k).start()

            @pl.when(mine)
            def _():
                yrecv[y] = ysend[k]

    for k in range(8):
        @pl.when(jnp.logical_not(y_self(k)))
        def _():
            remote(ysend.at[0], yrecv.at[k], y_s.at[0], y_r.at[k], (tm, row, col)).wait_recv()

    total = yrecv[0].astype(F32)
    for k in range(1, 8):
        total += yrecv[k].astype(F32)
    zsend[0:WIN] = total[0:WIN]
    zsend[WIN : WIN + 8] = total[WIN : WIN + 8] + total[WIN + 8 : WIN + 16]
    zsend[WIN + 8 :] = jnp.zeros((40, 128), F32)

    def z_copy(k):
        return remote(
            zsend.at[24 * k : 24 * k + 24], zrecv.at[z], z_s.at[k], z_r.at[z],
            (2 * x + k % 2, row, k // 2),
        )

    for k in range(8):
        @pl.when(z != k)
        def _():
            z_copy(k).start()

        @pl.when(z == k)
        def _():
            zrecv[k] = zsend[24 * k : 24 * k + 24]

    for k in range(8):
        @pl.when(z != k)
        def _():
            remote(zsend.at[0:24], zrecv.at[k], z_s.at[0], z_r.at[k], (tm, row, col)).wait_recv()

    total = zrecv[0]
    for k in range(1, 8):
        total += zrecv[k]
    bsend[...] = total

    def b_self(k):
        return jnp.logical_and(self_b, tm == k)

    def b_copy(k):
        return remote(bsend, brecv.at[z], b_s.at[k], b_r.at[z], (k, row, x))

    for k in range(8):
        @pl.when(jnp.logical_not(b_self(k)))
        def _():
            b_copy(k).start()

        @pl.when(b_self(k))
        def _():
            brecv[z] = bsend[...]

    for k in range(8):
        @pl.when(jnp.logical_not(jnp.logical_and(self_b, z == k)))
        def _():
            remote(bsend, brecv.at[k], b_s.at[0], b_r.at[k], (tm, row, col)).wait_recv()

    scale = 1.0 / math.sqrt(16 * 96 * 128)
    total = brecv[...].reshape(192, 128) * scale
    gg_out[...] = jnp.concatenate([total[WIN : WIN + 1], total[WIN + 1 : WIN + 2]], axis=1)
    fin[:, 0:128] = total[0:96]
    fin[0:48, 128:256] = total[96:WIN]
    fin[48:96, 128:256] = pltpu.roll(total[96:WIN], 64, 1)
    shard = row * 4 + col
    wg_out[...] = pltpu.roll(fin[...], (96 - shard % 16) % 96, 0)[0:81, 0:C]

    for copy in halo + swap + sent:
        copy.wait_send()
    for k in range(8):
        @pl.when(row != 8 * core + k)
        def _():
            y_copy(k).wait_send()

        @pl.when(z != k)
        def _():
            z_copy(k).wait_send()

        @pl.when(jnp.logical_not(b_self(k)))
        def _():
            b_copy(k).wait_send()


def per_device(features, cotangent, kernel, gain):
    vmem = pl.BlockSpec(memory_space=pltpu.VMEM)
    dma = pltpu.SemaphoreType.DMA
    fg, wg, gg = pl.pallas_call(
        body,
        out_shape=(
            jax.ShapeDtypeStruct((2, ROWS, COLS, C), BF16),
            jax.ShapeDtypeStruct((81, C), F32),
            jax.ShapeDtypeStruct((1, 256), F32),
        ),
        in_specs=[vmem, vmem, pl.BlockSpec(memory_space=pl.ANY), vmem],
        out_specs=(vmem, vmem, vmem),
        scratch_shapes=[
            pltpu.VMEM((27 * C, C), BF16),
            pltpu.VMEM((2, 3, 4, ROWS + 2, COLS, C), BF16),
            pltpu.VMEM((2, 2, 2, 3, 16, C), BF16),
            pltpu.VMEM((2, C, CELLS), BF16),
            pltpu.VMEM((2, 16, C), BF16),
            pltpu.VMEM((2, 16, C), F32),
            pltpu.VMEM((CELLS, 256), F32),
            pltpu.VMEM((8, 128), F32),
            pltpu.VMEM((HALF_TAPS * C + 96, 256), F32),
            pltpu.VMEM((4, 8 * WIN, 128), BF16),
            pltpu.VMEM((3, 8 * WIN, 128), BF16),
            pltpu.VMEM((2, 8, 128), F32),
            pltpu.VMEM((4, 8, 128), F32),
            pltpu.VMEM((8, WIN + 16, 128), BF16),
            pltpu.VMEM((8, WIN + 16, 128), BF16),
            pltpu.VMEM((192, 128), F32),
            pltpu.VMEM((8, 24, 128), F32),
            pltpu.VMEM((24, 128), F32),
            pltpu.VMEM((8, 24, 128), F32),
            pltpu.VMEM((96, 256), F32),
            dma(()),
            dma((17,)), dma((17,)), dma((3,)), dma((3,)),
            dma((PIECES, 3)), dma((PIECES, 3)), dma((4,)), dma((4,)),
            dma((8,)), dma((8,)), dma((8,)), dma((8,)), dma((8,)), dma((8,)),
        ],
        compiler_params=pltpu.CompilerParams(
            collective_id=0, has_side_effects=True, vmem_limit_bytes=48 * 1024 * 1024
        ),
    )(features, cotangent, kernel, gain.reshape(1, C))
    return fg, wg, gg[0, :C]


def solution(mesh):
    return jax.shard_map(
        per_device,
        mesh=mesh,
        in_specs=(P("tm", "row", "col", None), P("tm", "row", "col", None), P(), P()),
        out_specs=(P("tm", "row", "col", None), P(("row", "col"), None), P()),
        check_vma=False,
    )
```

```python
import math

import jax
import jax.numpy as jnp
from jax import lax
from jax.experimental import pallas as pl
from jax.experimental.pallas import tpu as pltpu
from jax.sharding import PartitionSpec as P

MESH = pl.DeviceIdType.MESH
F32 = jnp.float32
BF16 = jnp.bfloat16
C = 192
ROWS, COLS = 6, 32
CELLS = 2 * ROWS * COLS
HALF_TAPS = 14
SHARD = 81

HALO = [(1, 0, 0), (0, 1, 0), (1, 1, 0)]
HALO += [(df, out, dc) for df in (1, 0) for out in (0, 1) for dc in (-1, 1)]


def body(
    feat_hbm, cot_hbm, w_hbm, gain, fg_out, wg_out, gg_out,
    feat, cot, w_v, big, cols, act_t, packs, rows16, act32, wgl_a, wgl_b, xsend, xrecv,
    gpart, grecv_x, grecv_y, grecv_z, ysend, yrecv, zsend, zrecv, fin,
    in_sem, halo_s, halo_r, pair_s, pair_r, x_s, x_r, g_s, g_r, y_s, y_r, z_s, z_r, b_s, b_r,
):
    tm, row, col = lax.axis_index("tm"), lax.axis_index("row"), lax.axis_index("col")
    x, zlo = tm // 2, tm % 2
    y, core = row // 2, row % 2
    z = col * 2 + zlo
    other = 1 - core
    outward = 2 * core - 1
    partner = (tm, 2 * y + other, col)

    def near(dt, dr, dc):
        return ((tm + dt + 8) % 8, (row + dr + 16) % 16, (col + dc + 4) % 4)

    def x_dev(step):
        return (((x + step) % 4) * 2 + zlo, row, col)

    def y_dev(step):
        return (tm, (row + 2 * step) % 16, col)

    def z_dev(step):
        to = (z + step) % 8
        return (2 * x + to % 2, row, to // 2)

    def b_dev(step):
        return ((tm + step) % 8, row, col)

    def remote(src, dst, send, recv, device):
        return pltpu.make_async_remote_copy(
            src_ref=src, dst_ref=dst, send_sem=send, recv_sem=recv, device_id=device, device_id_type=MESH
        )

    main = big.at[0, 1]
    loads = [
        pltpu.make_async_copy(cot_hbm, cot, in_sem.at[0]),
        pltpu.make_async_copy(feat_hbm, feat, in_sem.at[1]),
        pltpu.make_async_copy(w_hbm, w_v, in_sem.at[2]),
    ]
    for copy in loads:
        copy.start()

    barrier = pltpu.get_barrier_semaphore()

    def greet(device):
        pl.semaphore_signal(barrier, inc=1, device_id=device, device_id_type=MESH)

    for df, out, dc in HALO:
        greet(near(df, outward * out, -dc))
    greet(partner)
    for step in range(1, 4):
        greet(x_dev(4 - step))
    for step in range(1, 8):
        greet(y_dev(8 - step))
        greet(z_dev(8 - step))
        greet(b_dev(8 - step))
    self_y = core == y // 4
    for k in range(8):
        @pl.when(jnp.logical_not(jnp.logical_and(self_y, y == k)))
        def _():
            greet((tm, 2 * k + y // 4, col))

    loads[0].wait()
    for side, q in ((0, 0), (1, COLS - 1)):
        rows16[side] = jnp.zeros((16, C), F32)
        for f in range(2):
            for r in range(ROWS):
                i = f * ROWS + r
                rows16[side, i : i + 1, :] = cot[f, r].astype(F32)[q : q + 1, :]
        packs[side] = rows16[side].astype(BF16)

    expected = len(HALO) + 1 + 3 + 7 + 7 + 7 + 8
    pl.semaphore_wait(barrier, expected - self_y.astype(jnp.int32))

    halo = []
    for m, (df, out, dc) in enumerate(HALO):
        if dc != 0:
            src = packs.at[0 if dc < 0 else 1]
            dst = cols.at[0, 1 if dc < 0 else 0, df, 2 * other if out else 1]
        elif out:
            src, dst = cot.at[:, (ROWS - 1) * core], main.at[2 * df : 2 * df + 2, (ROWS + 1) * other]
        else:
            src, dst = cot, main.at[2:4, 1 : ROWS + 1]
        halo.append(remote(src, dst, halo_s.at[m], halo_r.at[m], near(-df, outward * out, dc)))
        halo[-1].start()
    main[0:2, 1 : ROWS + 1] = cot[...]

    def norm():
        wide = feat[...].astype(F32).reshape(CELLS, C)
        inverse = lax.rsqrt(jnp.mean(wide * wide, axis=-1, keepdims=True) + 1e-06)
        normed = wide * inverse
        return inverse, normed, normed * gain[...]

    loads[1].wait()
    pre = norm()[2]
    act32[:, C:] = jnp.zeros((CELLS, 256 - C), F32)
    act32[:, :C] = pre * jax.nn.sigmoid(pre)
    act_t[0] = act32[...].T[:C].astype(BF16)
    swap = [remote(act_t.at[0], act_t.at[1], pair_s.at[0], pair_r.at[0], partner)]
    swap[0].start()

    for copy in halo:
        copy.wait_recv()

    @pl.when(row == 0)
    def _():
        main[:, 0] = jnp.zeros((4, COLS, C), BF16)
        cols[0, :, :, 0] = jnp.zeros((2, 2, 16, C), BF16)

    @pl.when(row == 15)
    def _():
        main[:, ROWS + 1] = jnp.zeros((4, COLS, C), BF16)
        cols[0, :, :, 2] = jnp.zeros((2, 2, 16, C), BF16)

    @pl.when(tm == 7)
    def _():
        main[2:4] = jnp.zeros((2, ROWS + 2, COLS, C), BF16)
        cols[0, :, 1] = jnp.zeros((2, 3, 16, C), BF16)

    @pl.when(col == 0)
    def _():
        cols[0, 0] = jnp.zeros((2, 3, 16, C), BF16)

    @pl.when(col == 3)
    def _():
        cols[0, 1] = jnp.zeros((2, 3, 16, C), BF16)

    swap.append(remote(main, big.at[1, 1], pair_s.at[1], pair_r.at[1], partner))
    swap.append(remote(cols.at[0], cols.at[1], pair_s.at[2], pair_r.at[2], partner))
    swap[1].start()
    swap[2].start()
    for copy in swap:
        copy.wait()
    main[:, (ROWS + 1) * other] = big[1, 1, :, 1 + (ROWS - 1) * core]
    big[1, 1, :, (ROWS + 1) * core] = main[:, ROWS - (ROWS - 1) * core]
    cols[0, :, :, 2 * other] = cols[1, :, :, 1]
    cols[1, :, :, 2 * core] = cols[0, :, :, 1]

    spot = lax.broadcasted_iota(jnp.int32, (COLS, C), 0)

    def shift(tile):
        for f in range(4):
            edges = [[cols[tile, s, f // 2, k].astype(F32) for k in range(3)] for s in (0, 1)]
            for r in range(ROWS + 2):
                k = 0 if r == 0 else 2 if r == ROWS + 1 else 1
                i = (f % 2) * ROWS + (r - 1) % ROWS
                value = big[tile, 1, f, r].astype(F32)
                after = jnp.where(spot == COLS - 1, edges[1][k][i : i + 1], pltpu.roll(value, COLS - 1, 0))
                before = jnp.where(spot == 0, edges[0][k][i : i + 1], pltpu.roll(value, 1, 0))
                big[tile, 0, f, r] = after.astype(BF16)
                big[tile, 2, f, r] = before.astype(BF16)

    shift(0)
    shift(1)

    for i in range(HALF_TAPS):
        tap = i + 13 * core
        a, b, c = tap // 9, (tap // 3) % 3, tap % 3
        total = jnp.zeros((C, C), F32)
        for tile in (0, 1):
            patch = big[tile, c, pl.ds(2 - a, 2), pl.ds(2 - b, ROWS)].reshape(CELLS, C)
            total += jnp.dot(act_t[tile], patch, preferred_element_type=F32)
        at = pl.multiple_of(i * C + 96 * other, 8)
        wgl_a[pl.ds(at, C), :] = total[:, 0:128]
        wgl_b[pl.ds(at, C), 0:64] = total[:, 128:C]

    lane = lax.broadcasted_iota(jnp.int32, (40, 128), 1)
    line = lax.broadcasted_iota(jnp.int32, (88, 128), 0)
    for j in range(32):
        at = 96 + SHARD * j
        upper = jnp.where(
            line < SHARD, wgl_a[at : at + 88], jnp.where(line == SHARD, wgl_b[at + 80 : at + 81], 0.0)
        )
        lower = jnp.where(lane < 64, wgl_b[at : at + 40], pltpu.roll(wgl_b[at + 40 : at + 80], 64, 1))
        value = jnp.concatenate([upper, lower], axis=0).astype(BF16)
        for k in range(4):
            xsend[k, j % 4, 32 * (j // 4) : 32 * (j // 4) + 32] = value[32 * k : 32 * k + 32]

    def x_copy(w, step):
        return remote(
            xsend.at[(x + step) % 4, w], xrecv.at[step - 1, w],
            x_s.at[w, step - 1], x_r.at[w, step - 1], x_dev(step),
        )

    def x_start(w):
        for step in (1, 2, 3):
            x_copy(w, step).start()

    x_start(0)
    x_start(1)

    loads[2].wait()
    dact = jnp.zeros((CELLS, C), F32)
    for tap in range(27):
        a, b, c = tap // 9, (tap // 3) % 3, tap % 3
        patch = big[0, c, 2 - a : 4 - a, 2 - b : 2 - b + ROWS].reshape(CELLS, C)
        dact += jnp.dot(patch, w_v[:, tap * C : (tap + 1) * C], preferred_element_type=F32)
    inverse, normed, pre = norm()
    sigma = jax.nn.sigmoid(pre)
    dpre = dact * sigma * (1.0 + pre * (1.0 - sigma))
    gain_part = jnp.sum(dpre * normed, axis=0, keepdims=True)
    dnormed = dpre * gain[...]
    project = jnp.mean(dnormed * normed, axis=-1, keepdims=True)
    grad = cot[...].astype(F32).reshape(CELLS, C) + inverse * (dnormed - normed * project)
    fg_out[...] = grad.astype(BF16).reshape(2, ROWS, COLS, C)

    act32[0:8, :] = jnp.zeros((8, 256), F32)
    act32[0:1, :C] = gain_part
    gpart[0] = act32[0:8, 0:128]
    gpart[0, 1:2] = act32[0:1, 128:256]
    gain_steps = [
        [remote(gpart.at[0], grecv_x.at[0], g_s.at[0], g_r.at[0], partner)],
        [remote(gpart.at[1], grecv_x.at[k], g_s.at[k], g_r.at[k], x_dev(k)) for k in range(1, 4)],
        [remote(gpart.at[2], grecv_y.at[k - 1], g_s.at[3 + k], g_r.at[3 + k], y_dev(k)) for k in range(1, 8)],
        [remote(gpart.at[3], grecv_z.at[k - 1], g_s.at[10 + k], g_r.at[10 + k], z_dev(k)) for k in range(1, 8)],
    ]

    def gain_begin(n):
        for copy in gain_steps[n]:
            copy.start()

    def gain_end(n):
        for copy in gain_steps[n]:
            copy.wait()
        total = gpart[n]
        arrived = [grecv_x[0:1], grecv_x[1:4], grecv_y[...], grecv_z[...]][n]
        for k in range(len(gain_steps[n])):
            total += arrived[k]
        gpart[n + 1] = total

    gain_begin(0)

    def y_copy(w, k):
        return remote(
            ysend.at[w, 32 * k : 32 * k + 32], yrecv.at[w, y], y_s.at[w, k], y_r.at[w, y],
            (tm, 8 * core + k, col),
        )

    def z_copy(w, k):
        return remote(
            zsend.at[w, 16 * k : 16 * k + 16], zrecv.at[z], z_s.at[w, k], z_r.at[z], (2 * x + k, row, w)
        )

    def over_y(w):
        for step in (1, 2, 3):
            x_copy(w, step).wait()
        if w + 2 < 4:
            x_start(w + 2)
        value = xsend[x, w].astype(F32)
        for step in (1, 2, 3):
            value += xrecv[step - 1, w].astype(F32)
        ysend[w] = value.astype(BF16)
        for k in range(8):
            mine = row == 8 * core + k

            @pl.when(jnp.logical_not(mine))
            def _():
                y_copy(w, k).start()

            @pl.when(mine)
            def _():
                yrecv[w, y] = ysend[w, 32 * k : 32 * k + 32]

    def over_z(w):
        for k in range(8):
            @pl.when(jnp.logical_not(jnp.logical_and(self_y, y == k)))
            def _():
                remote(ysend.at[w, 0:32], yrecv.at[w, k], y_s.at[w, 0], y_r.at[w, k], partner).wait_recv()

        total = yrecv[w, 0].astype(F32)
        for k in range(1, 8):
            total += yrecv[w, k].astype(F32)
        zsend[w] = total
        for k in range(2):
            @pl.when(z != 2 * w + k)
            def _():
                z_copy(w, k).start()

            @pl.when(z == 2 * w + k)
            def _():
                zrecv[z] = zsend[w, 16 * k : 16 * k + 16]

    over_y(0)
    gain_end(0)
    gain_begin(1)
    over_y(1)
    over_z(0)
    gain_end(1)
    gain_begin(2)
    over_y(2)
    over_z(1)
    gain_end(2)
    gain_begin(3)
    over_y(3)
    over_z(2)
    over_z(3)
    gain_end(3)

    for k in range(8):
        @pl.when(z != k)
        def _():
            remote(zsend.at[0, 0:16], zrecv.at[k], z_s.at[0, 0], z_r.at[k], partner).wait_recv()

    total = zrecv[0]
    for k in range(1, 8):
        total += zrecv[k]
    fin[tm] = total

    last = []
    for step in range(1, 8):
        last.append(remote(fin.at[tm], fin.at[tm], b_s.at[step - 1], b_r.at[step - 1], b_dev(step)))
        last[-1].start()
    for copy in last:
        copy.wait()

    scale = 1.0 / math.sqrt(16 * 96 * 128)
    gain_total = gpart[4] * scale
    gg_out[...] = jnp.concatenate([gain_total[0:1], gain_total[1:2]], axis=1)
    value = fin[...].reshape(128, 128) * scale
    wg_out[:, 0:128] = value[0:SHARD]
    wg_out[0:40, 128:C] = value[88:128, 0:64]
    wg_out[40:80, 128:C] = pltpu.roll(value[88:128], 64, 1)[:, 0:64]
    wg_out[80:81, 128:C] = value[81:82, 0:64]

    for copy in halo:
        copy.wait_send()
    for w in range(4):
        for k in range(8):
            @pl.when(row != 8 * core + k)
            def _():
                y_copy(w, k).wait_send()

        for k in range(2):
            @pl.when(z != 2 * w + k)
            def _():
                z_copy(w, k).wait_send()


def per_device(features, cotangent, kernel, gain):
    vmem = pl.BlockSpec(memory_space=pltpu.VMEM)
    hbm = pl.BlockSpec(memory_space=pltpu.HBM)
    dma = pltpu.SemaphoreType.DMA
    fg, wg, gg = pl.pallas_call(
        body,
        out_shape=(
            jax.ShapeDtypeStruct((2, ROWS, COLS, C), BF16),
            jax.ShapeDtypeStruct((SHARD, C), F32),
            jax.ShapeDtypeStruct((1, 256), F32),
        ),
        in_specs=[hbm, hbm, hbm, vmem],
        out_specs=(vmem, vmem, vmem),
        scratch_shapes=[
            pltpu.VMEM((2, ROWS, COLS, C), BF16),
            pltpu.VMEM((2, ROWS, COLS, C), BF16),
            pltpu.VMEM((C, 27 * C), BF16),
            pltpu.VMEM((2, 3, 4, ROWS + 2, COLS, C), BF16),
            pltpu.VMEM((2, 2, 2, 3, 16, C), BF16),
            pltpu.VMEM((2, C, CELLS), BF16),
            pltpu.VMEM((2, 16, C), BF16),
            pltpu.VMEM((2, 16, C), F32),
            pltpu.VMEM((CELLS, 256), F32),
            pltpu.VMEM((HALF_TAPS * C + 96, 128), F32),
            pltpu.VMEM((HALF_TAPS * C + 96, 128), F32),
            pltpu.VMEM((4, 4, 256, 128), BF16),
            pltpu.VMEM((3, 4, 256, 128), BF16),
            pltpu.VMEM((5, 8, 128), F32),
            pltpu.VMEM((4, 8, 128), F32),
            pltpu.VMEM((7, 8, 128), F32),
            pltpu.VMEM((7, 8, 128), F32),
            pltpu.VMEM((4, 256, 128), BF16),
            pltpu.VMEM((4, 8, 32, 128), BF16),
            pltpu.VMEM((4, 32, 128), F32),
            pltpu.VMEM((8, 16, 128), F32),
            pltpu.VMEM((8, 16, 128), F32),
            dma((3,)),
            dma((len(HALO),)), dma((len(HALO),)), dma((3,)), dma((3,)),
            dma((4, 3)), dma((4, 3)), dma((18,)), dma((18,)),
            dma((4, 8)), dma((4, 8)), dma((4, 2)), dma((8,)), dma((7,)), dma((7,)),
        ],
        compiler_params=pltpu.CompilerParams(
            collective_id=0, has_side_effects=True, vmem_limit_bytes=48 * 1024 * 1024
        ),
    )(features, cotangent, kernel.T, gain.reshape(1, C))
    return fg, wg, gg[0, :C]


def solution(mesh):
    return jax.shard_map(
        per_device,
        mesh=mesh,
        in_specs=(P("tm", "row", "col", None), P("tm", "row", "col", None), P(), P()),
        out_specs=(P("tm", "row", "col", None), P(("row", "col"), None), P()),
        check_vma=False,
    )
```

```python
import math

import jax
import jax.numpy as jnp
from jax import lax
from jax.experimental import pallas as pl
from jax.experimental.pallas import tpu as pltpu
from jax.sharding import PartitionSpec as P

MESH = pl.DeviceIdType.MESH
F32 = jnp.float32
BF16 = jnp.bfloat16
C = 192
ROWS, COLS = 6, 32
CELLS = 2 * ROWS * COLS
LATE, EARLY = 11, 4
SHARD = 81

HALO = [(0, 1, 0)] + [(0, out, dc) for out in (0, 1) for dc in (-1, 1)]
HALO += [(1, 0, 0), (1, 1, 0)] + [(1, out, dc) for out in (0, 1) for dc in (-1, 1)]
NOW = 5


def body(
    feat_hbm, cot_hbm, w_hbm, gain, fg_out, wg_out, gg_out,
    feat, cot, w_v, big, cols, act_t, packs, rows16, act32, wgl_a, wgl_b, xsend, xrecv, esend, erecv,
    gpart, grecv_x, grecv_y, grecv_z, ysend, yrecv, zsend, zrecv, fin,
    in_sem, halo_s, halo_r, pair_s, pair_r, x_s, x_r, e_s, e_r, g_s, g_r, y_s, y_r, z_s, z_r, b_s, b_r,
):
    tm, row, col = lax.axis_index("tm"), lax.axis_index("row"), lax.axis_index("col")
    x, zlo = tm // 2, tm % 2
    y, core = row // 2, row % 2
    z = col * 2 + zlo
    other = 1 - core
    outward = 2 * core - 1
    partner = (tm, 2 * y + other, col)

    def near(dt, dr, dc):
        return ((tm + dt + 8) % 8, (row + dr + 16) % 16, (col + dc + 4) % 4)

    def x_dev(step):
        return (((x + step) % 4) * 2 + zlo, row, col)

    def y_dev(step):
        return (tm, (row + 2 * step) % 16, col)

    def z_dev(step):
        to = (z + step) % 8
        return (2 * x + to % 2, row, to // 2)

    def b_dev(step):
        return ((tm + step) % 8, row, col)

    def remote(src, dst, send, recv, device):
        return pltpu.make_async_remote_copy(
            src_ref=src, dst_ref=dst, send_sem=send, recv_sem=recv, device_id=device, device_id_type=MESH
        )

    main = big.at[0, 1]
    loads = [
        pltpu.make_async_copy(cot_hbm, cot, in_sem.at[0]),
        pltpu.make_async_copy(feat_hbm, feat, in_sem.at[1]),
        pltpu.make_async_copy(w_hbm, w_v, in_sem.at[2]),
    ]
    for copy in loads:
        copy.start()

    barrier = pltpu.get_barrier_semaphore()

    def greet(device):
        pl.semaphore_signal(barrier, inc=1, device_id=device, device_id_type=MESH)

    for df, out, dc in HALO:
        greet(near(df, outward * out, -dc))
    greet(partner)
    for step in range(1, 4):
        greet(x_dev(4 - step))
    for step in range(1, 8):
        greet(y_dev(8 - step))
        greet(z_dev(8 - step))
        greet(b_dev(8 - step))
    holder = jnp.logical_and(row >= 6, row < 14).astype(jnp.int32)
    self_y = core == holder
    for k in range(8):
        @pl.when(jnp.logical_not(jnp.logical_and(self_y, y == k)))
        def _():
            greet((tm, 2 * k + holder, col))

    loads[0].wait()
    for side, q in ((0, 0), (1, COLS - 1)):
        rows16[side] = jnp.zeros((16, C), F32)
        for f in range(2):
            for r in range(ROWS):
                i = f * ROWS + r
                rows16[side, i : i + 1, :] = cot[f, r].astype(F32)[q : q + 1, :]
        packs[side] = rows16[side].astype(BF16)

    expected = len(HALO) + 1 + 3 + 7 + 7 + 7 + 8
    pl.semaphore_wait(barrier, expected - self_y.astype(jnp.int32))

    halo = []
    for m, (df, out, dc) in enumerate(HALO):
        if dc != 0:
            src = packs.at[0 if dc < 0 else 1]
            dst = cols.at[0, df, 1 if dc < 0 else 0, 2 * other if out else 1]
        elif out:
            src, dst = cot.at[:, (ROWS - 1) * core], main.at[2 * df : 2 * df + 2, (ROWS + 1) * other]
        else:
            src, dst = cot, main.at[2:4, 1 : ROWS + 1]
        halo.append(remote(src, dst, halo_s.at[m], halo_r.at[m], near(-df, outward * out, dc)))
        halo[-1].start()
    main[0:2, 1 : ROWS + 1] = cot[...]

    def norm():
        wide = feat[...].astype(F32).reshape(CELLS, C)
        inverse = lax.rsqrt(jnp.mean(wide * wide, axis=-1, keepdims=True) + 1e-06)
        normed = wide * inverse
        return inverse, normed, normed * gain[...]

    loads[1].wait()
    pre = norm()[2]
    act32[:, C:] = jnp.zeros((CELLS, 256 - C), F32)
    act32[:, :C] = pre * jax.nn.sigmoid(pre)
    act_t[0] = act32[...].T[:C].astype(BF16)
    swap = [remote(act_t.at[0], act_t.at[1], pair_s.at[0], pair_r.at[0], partner)]
    swap[0].start()

    other_main = big.at[1, 1]

    def borders(df):
        f = slice(2 * df, 2 * df + 2)
        for copy in halo[:NOW] if df == 0 else halo[NOW:]:
            copy.wait_recv()

        @pl.when(row == 0)
        def _():
            main[f, 0] = jnp.zeros((2, COLS, C), BF16)
            cols[0, df, :, 0] = jnp.zeros((2, 16, C), BF16)

        @pl.when(row == 15)
        def _():
            main[f, ROWS + 1] = jnp.zeros((2, COLS, C), BF16)
            cols[0, df, :, 2] = jnp.zeros((2, 16, C), BF16)

        if df == 1:
            @pl.when(tm == 7)
            def _():
                main[f] = jnp.zeros((2, ROWS + 2, COLS, C), BF16)
                cols[0, df] = jnp.zeros((2, 3, 16, C), BF16)

        @pl.when(col == 0)
        def _():
            cols[0, df, 0] = jnp.zeros((3, 16, C), BF16)

        @pl.when(col == 3)
        def _():
            cols[0, df, 1] = jnp.zeros((3, 16, C), BF16)

        for copy in [
            remote(main.at[f], other_main.at[f], pair_s.at[1 + 2 * df], pair_r.at[1 + 2 * df], partner),
            remote(cols.at[0, df], cols.at[1, df], pair_s.at[2 + 2 * df], pair_r.at[2 + 2 * df], partner),
        ]:
            copy.start()
            swap.append(copy)
        for copy in swap:
            copy.wait()
        swap.clear()
        main[f, (ROWS + 1) * other] = big[1, 1, f, 1 + (ROWS - 1) * core]
        other_main[f, (ROWS + 1) * core] = main[f, ROWS - (ROWS - 1) * core]
        cols[0, df, :, 2 * other] = cols[1, df, :, 1]
        cols[1, df, :, 2 * core] = cols[0, df, :, 1]

    spot = lax.broadcasted_iota(jnp.int32, (COLS, C), 0)

    def shift(tile, df):
        edges = [[cols[tile, df, s, k].astype(F32) for k in range(3)] for s in (0, 1)]
        for f in (2 * df, 2 * df + 1):
            for r in range(ROWS + 2):
                k = 0 if r == 0 else 2 if r == ROWS + 1 else 1
                i = (f % 2) * ROWS + (r - 1) % ROWS
                value = big[tile, 1, f, r].astype(F32)
                after = jnp.where(spot == COLS - 1, edges[1][k][i : i + 1], pltpu.roll(value, COLS - 1, 0))
                before = jnp.where(spot == 0, edges[0][k][i : i + 1], pltpu.roll(value, 1, 0))
                big[tile, 0, f, r] = after.astype(BF16)
                big[tile, 2, f, r] = before.astype(BF16)

    def tap_grad(tap, at):
        a, b, c = tap // 9, (tap // 3) % 3, tap % 3
        total = jnp.zeros((C, C), F32)
        for tile in (0, 1):
            patch = big[tile, c, pl.ds(2 - a, 2), pl.ds(2 - b, ROWS)].reshape(CELLS, C)
            total += jnp.dot(act_t[tile], patch, preferred_element_type=F32)
        at = pl.multiple_of(at, 8)
        wgl_a[pl.ds(at, C), :] = total[:, 0:128]
        wgl_b[pl.ds(at, C), 0:64] = total[:, 128:C]

    lane = lax.broadcasted_iota(jnp.int32, (40, 128), 1)
    line = lax.broadcasted_iota(jnp.int32, (88, 128), 0)

    def pack(at):
        upper = jnp.where(
            line < SHARD, wgl_a[at : at + 88], jnp.where(line == SHARD, wgl_b[at + 80 : at + 81], 0.0)
        )
        lower = jnp.where(lane < 64, wgl_b[at : at + 40], pltpu.roll(wgl_b[at + 40 : at + 80], 64, 1))
        return jnp.concatenate([upper, lower], axis=0).astype(BF16)

    def e_copy(step):
        return remote(
            esend.at[(x + step) % 4], erecv.at[step - 1], e_s.at[step - 1], e_r.at[step - 1], x_dev(step)
        )

    borders(0)
    shift(0, 0)
    shift(1, 0)
    base = LATE * C + 24
    for i in range(EARLY):
        tap_grad(23 - 3 * core + i, base + i * C + 72 * core)
    for j in range(8):
        value = pack(base + 120 + SHARD * j)
        at = 64 * (j % 4) + 32 * (j // 4)
        for k in range(4):
            esend[k, at : at + 32] = value[32 * k : 32 * k + 32]
    for step in (1, 2, 3):
        e_copy(step).start()

    borders(1)
    shift(0, 1)
    shift(1, 1)
    for i in range(LATE):
        tap_grad(10 * core + i, i * C + 24 * other)
    for j in range(24):
        value = pack(24 + SHARD * j)
        for k in range(4):
            xsend[k, j % 4, 32 * (j // 4) : 32 * (j // 4) + 32] = value[32 * k : 32 * k + 32]

    def x_copy(w, step):
        return remote(
            xsend.at[(x + step) % 4, w], xrecv.at[step - 1, w],
            x_s.at[w, step - 1], x_r.at[w, step - 1], x_dev(step),
        )

    def x_start(w):
        for step in (1, 2, 3):
            x_copy(w, step).start()

    x_start(0)
    x_start(1)

    loads[2].wait()
    dact = jnp.zeros((CELLS, C), F32)
    for tap in range(27):
        a, b, c = tap // 9, (tap // 3) % 3, tap % 3
        patch = big[0, c, 2 - a : 4 - a, 2 - b : 2 - b + ROWS].reshape(CELLS, C)
        dact += jnp.dot(patch, w_v[:, tap * C : (tap + 1) * C], preferred_element_type=F32)
    inverse, normed, pre = norm()
    sigma = jax.nn.sigmoid(pre)
    dpre = dact * sigma * (1.0 + pre * (1.0 - sigma))
    gain_part = jnp.sum(dpre * normed, axis=0, keepdims=True)
    dnormed = dpre * gain[...]
    project = jnp.mean(dnormed * normed, axis=-1, keepdims=True)
    grad = cot[...].astype(F32).reshape(CELLS, C) + inverse * (dnormed - normed * project)
    fg_out[...] = grad.astype(BF16).reshape(2, ROWS, COLS, C)

    act32[0:8, :] = jnp.zeros((8, 256), F32)
    act32[0:1, :C] = gain_part
    gpart[0] = act32[0:8, 0:128]
    gpart[0, 1:2] = act32[0:1, 128:256]
    gain_steps = [
        [remote(gpart.at[0], grecv_x.at[0], g_s.at[0], g_r.at[0], partner)],
        [remote(gpart.at[1], grecv_x.at[k], g_s.at[k], g_r.at[k], x_dev(k)) for k in range(1, 4)],
        [remote(gpart.at[2], grecv_y.at[k - 1], g_s.at[3 + k], g_r.at[3 + k], y_dev(k)) for k in range(1, 8)],
        [remote(gpart.at[3], grecv_z.at[k - 1], g_s.at[10 + k], g_r.at[10 + k], z_dev(k)) for k in range(1, 8)],
    ]

    def gain_begin(n):
        for copy in gain_steps[n]:
            copy.start()

    def gain_end(n):
        for copy in gain_steps[n]:
            copy.wait()
        total = gpart[n]
        arrived = [grecv_x[0:1], grecv_x[1:4], grecv_y[...], grecv_z[...]][n]
        for k in range(len(gain_steps[n])):
            total += arrived[k]
        gpart[n + 1] = total

    gain_begin(0)

    def y_row(k):
        return k + 6 * core if k < 6 else k + 8 - 2 * core

    def y_copy(w, k):
        return remote(
            ysend.at[w, 32 * k : 32 * k + 32], yrecv.at[w, y], y_s.at[w, k], y_r.at[w, y],
            (tm, y_row(k), col),
        )

    def z_copy(w, k):
        return remote(
            zsend.at[w, 16 * k : 16 * k + 16], zrecv.at[z], z_s.at[w, k], z_r.at[z], (2 * x + k, row, w)
        )

    def over_y(w):
        for step in (1, 2, 3):
            x_copy(w, step).wait()
        if w + 2 < 4:
            x_start(w + 2)
        part = slice(64 * w, 64 * w + 64)
        value = xsend[x, w].astype(F32)
        extra = esend[x, part].astype(F32)
        for step in (1, 2, 3):
            value += xrecv[step - 1, w].astype(F32)
            extra += erecv[step - 1, part].astype(F32)
        ysend[w, 0:192] = value.astype(BF16)
        ysend[w, 192:256] = extra.astype(BF16)
        for k in range(8):
            mine = row == y_row(k)

            @pl.when(jnp.logical_not(mine))
            def _():
                y_copy(w, k).start()

            @pl.when(mine)
            def _():
                yrecv[w, y] = ysend[w, 32 * k : 32 * k + 32]

    def over_z(w):
        for k in range(8):
            @pl.when(jnp.logical_not(jnp.logical_and(self_y, y == k)))
            def _():
                remote(ysend.at[w, 0:32], yrecv.at[w, k], y_s.at[w, 0], y_r.at[w, k], partner).wait_recv()

        total = yrecv[w, 0].astype(F32)
        for k in range(1, 8):
            total += yrecv[w, k].astype(F32)
        zsend[w] = total
        for k in range(2):
            @pl.when(z != 2 * w + k)
            def _():
                z_copy(w, k).start()

            @pl.when(z == 2 * w + k)
            def _():
                zrecv[z] = zsend[w, 16 * k : 16 * k + 16]

    for step in (1, 2, 3):
        e_copy(step).wait()
    over_y(0)
    gain_end(0)
    gain_begin(1)
    over_y(1)
    over_z(0)
    gain_end(1)
    gain_begin(2)
    over_y(2)
    over_z(1)
    gain_end(2)
    gain_begin(3)
    over_y(3)
    over_z(2)
    over_z(3)
    gain_end(3)

    for k in range(8):
        @pl.when(z != k)
        def _():
            remote(zsend.at[0, 0:16], zrecv.at[k], z_s.at[0, 0], z_r.at[k], partner).wait_recv()

    total = zrecv[0]
    for k in range(1, 8):
        total += zrecv[k]
    fin[tm] = total

    last = []
    for step in range(1, 8):
        last.append(remote(fin.at[tm], fin.at[tm], b_s.at[step - 1], b_r.at[step - 1], b_dev(step)))
        last[-1].start()
    for copy in last:
        copy.wait()

    scale = 1.0 / math.sqrt(16 * 96 * 128)
    gain_total = gpart[4] * scale
    gg_out[...] = jnp.concatenate([gain_total[0:1], gain_total[1:2]], axis=1)
    value = fin[...].reshape(128, 128) * scale
    wg_out[:, 0:128] = value[0:SHARD]
    wg_out[0:40, 128:C] = value[88:128, 0:64]
    wg_out[40:80, 128:C] = pltpu.roll(value[88:128], 64, 1)[:, 0:64]
    wg_out[80:81, 128:C] = value[81:82, 0:64]

    for copy in halo:
        copy.wait_send()
    for w in range(4):
        for k in range(8):
            @pl.when(row != y_row(k))
            def _():
                y_copy(w, k).wait_send()

        for k in range(2):
            @pl.when(z != 2 * w + k)
            def _():
                z_copy(w, k).wait_send()


def per_device(features, cotangent, kernel, gain):
    vmem = pl.BlockSpec(memory_space=pltpu.VMEM)
    hbm = pl.BlockSpec(memory_space=pltpu.HBM)
    dma = pltpu.SemaphoreType.DMA
    fg, wg, gg = pl.pallas_call(
        body,
        out_shape=(
            jax.ShapeDtypeStruct((2, ROWS, COLS, C), BF16),
            jax.ShapeDtypeStruct((SHARD, C), F32),
            jax.ShapeDtypeStruct((1, 256), F32),
        ),
        in_specs=[hbm, hbm, hbm, vmem],
        out_specs=(vmem, vmem, vmem),
        scratch_shapes=[
            pltpu.VMEM((2, ROWS, COLS, C), BF16),
            pltpu.VMEM((2, ROWS, COLS, C), BF16),
            pltpu.VMEM((C, 27 * C), BF16),
            pltpu.VMEM((2, 3, 4, ROWS + 2, COLS, C), BF16),
            pltpu.VMEM((2, 2, 2, 3, 16, C), BF16),
            pltpu.VMEM((2, C, CELLS), BF16),
            pltpu.VMEM((2, 16, C), BF16),
            pltpu.VMEM((2, 16, C), F32),
            pltpu.VMEM((CELLS, 256), F32),
            pltpu.VMEM(((LATE + EARLY) * C + 96, 128), F32),
            pltpu.VMEM(((LATE + EARLY) * C + 96, 128), F32),
            pltpu.VMEM((4, 4, 192, 128), BF16),
            pltpu.VMEM((3, 4, 192, 128), BF16),
            pltpu.VMEM((4, 256, 128), BF16),
            pltpu.VMEM((3, 256, 128), BF16),
            pltpu.VMEM((5, 8, 128), F32),
            pltpu.VMEM((4, 8, 128), F32),
            pltpu.VMEM((7, 8, 128), F32),
            pltpu.VMEM((7, 8, 128), F32),
            pltpu.VMEM((4, 256, 128), BF16),
            pltpu.VMEM((4, 8, 32, 128), BF16),
            pltpu.VMEM((4, 32, 128), F32),
            pltpu.VMEM((8, 16, 128), F32),
            pltpu.VMEM((8, 16, 128), F32),
            dma((3,)),
            dma((len(HALO),)), dma((len(HALO),)), dma((5,)), dma((5,)),
            dma((4, 3)), dma((4, 3)), dma((3,)), dma((3,)), dma((18,)), dma((18,)),
            dma((4, 8)), dma((4, 8)), dma((4, 2)), dma((8,)), dma((7,)), dma((7,)),
        ],
        compiler_params=pltpu.CompilerParams(
            collective_id=0, has_side_effects=True, vmem_limit_bytes=64 * 1024 * 1024 - 65536
        ),
    )(features, cotangent, kernel.T, gain.reshape(1, C))
    return fg, wg, gg[0, :C]


def solution(mesh):
    return jax.shard_map(
        per_device,
        mesh=mesh,
        in_specs=(P("tm", "row", "col", None), P("tm", "row", "col", None), P(), P()),
        out_specs=(P("tm", "row", "col", None), P(("row", "col"), None), P()),
        check_vma=False,
    )
```

```python
import math

import jax
import jax.numpy as jnp
from jax import lax
from jax.experimental import pallas as pl
from jax.experimental.pallas import tpu as pltpu
from jax.sharding import PartitionSpec as P

MESH = pl.DeviceIdType.MESH
F32 = jnp.float32
BF16 = jnp.bfloat16
C = 192
ROWS, COLS = 6, 32
CELLS = 2 * ROWS * COLS
LATE, EARLY = 11, 4
SHARD = 81

HALO = [(0, 1, 0)] + [(0, out, dc) for out in (0, 1) for dc in (-1, 1)]
HALO += [(1, 0, 0), (1, 1, 0)] + [(1, out, dc) for out in (0, 1) for dc in (-1, 1)]
NOW = 5


def body(
    feat_hbm, cot_hbm, w_hbm, gain, fg_out, wg_out, gg_out,
    feat, cot, w_v, big, cols, act_t, packs, rows16, act32, wgl_a, wgl_b, xsend, xrecv, esend, erecv, fsend, frecv, htotal, hsend, hrecv,
    gpart, grecv_x, grecv_y, grecv_z, ysend, yrecv, zsend, zrecv, fin,
    in_sem, halo_s, halo_r, pair_s, pair_r, x_s, x_r, e_s, e_r, f_s, f_r, h_s, h_r, g_s, g_r, y_s, y_r, z_s, z_r, b_s, b_r,
):
    tm, row, col = lax.axis_index("tm"), lax.axis_index("row"), lax.axis_index("col")
    x, zlo = tm // 2, tm % 2
    y, core = row // 2, row % 2
    z = col * 2 + zlo
    other = 1 - core
    outward = 2 * core - 1
    partner = (tm, 2 * y + other, col)

    def near(dt, dr, dc):
        return ((tm + dt + 8) % 8, (row + dr + 16) % 16, (col + dc + 4) % 4)

    def x_dev(step):
        return (((x + step) % 4) * 2 + zlo, row, col)

    def y_dev(step):
        return (tm, (row + 2 * step) % 16, col)

    def z_dev(step):
        to = (z + step) % 8
        return (2 * x + to % 2, row, to // 2)

    def b_dev(step):
        return ((tm + step) % 8, row, col)

    def remote(src, dst, send, recv, device):
        return pltpu.make_async_remote_copy(
            src_ref=src, dst_ref=dst, send_sem=send, recv_sem=recv, device_id=device, device_id_type=MESH
        )

    main = big.at[0, 1]
    loads = [
        pltpu.make_async_copy(cot_hbm, cot, in_sem.at[0]),
        pltpu.make_async_copy(feat_hbm, feat, in_sem.at[1]),
        pltpu.make_async_copy(w_hbm, w_v, in_sem.at[2]),
    ]
    for copy in loads:
        copy.start()

    barrier = pltpu.get_barrier_semaphore()

    def greet(device):
        pl.semaphore_signal(barrier, inc=1, device_id=device, device_id_type=MESH)

    for df, out, dc in HALO:
        greet(near(df, outward * out, -dc))
    greet(partner)
    for step in range(1, 4):
        greet(x_dev(4 - step))
    for step in range(1, 8):
        greet(y_dev(8 - step))
        greet(z_dev(8 - step))
        greet(b_dev(8 - step))
    holder = jnp.logical_and(row >= 6, row < 14).astype(jnp.int32)
    self_y = core == holder
    for k in range(8):
        @pl.when(jnp.logical_not(jnp.logical_and(self_y, y == k)))
        def _():
            greet((tm, 2 * k + holder, col))

    loads[0].wait()
    for side, q in ((0, 0), (1, COLS - 1)):
        rows16[side] = jnp.zeros((16, C), F32)
        for f in range(2):
            for r in range(ROWS):
                i = f * ROWS + r
                rows16[side, i : i + 1, :] = cot[f, r].astype(F32)[q : q + 1, :]
        packs[side] = rows16[side].astype(BF16)

    expected = len(HALO) + 1 + 3 + 7 + 7 + 7 + 8
    pl.semaphore_wait(barrier, expected - self_y.astype(jnp.int32))

    halo = []
    for m, (df, out, dc) in enumerate(HALO):
        if dc != 0:
            src = packs.at[0 if dc < 0 else 1]
            dst = cols.at[0, df, 1 if dc < 0 else 0, 2 * other if out else 1]
        elif out:
            src, dst = cot.at[:, (ROWS - 1) * core], main.at[2 * df : 2 * df + 2, (ROWS + 1) * other]
        else:
            src, dst = cot, main.at[2:4, 1 : ROWS + 1]
        halo.append(remote(src, dst, halo_s.at[m], halo_r.at[m], near(-df, outward * out, dc)))
        halo[-1].start()
    main[0:2, 1 : ROWS + 1] = cot[...]

    def norm():
        wide = feat[...].astype(F32).reshape(CELLS, C)
        inverse = lax.rsqrt(jnp.mean(wide * wide, axis=-1, keepdims=True) + 1e-06)
        normed = wide * inverse
        return inverse, normed, normed * gain[...]

    loads[1].wait()
    pre = norm()[2]
    act32[:, C:] = jnp.zeros((CELLS, 256 - C), F32)
    act32[:, :C] = pre * jax.nn.sigmoid(pre)
    act_t[0] = act32[...].T[:C].astype(BF16)
    swap = [remote(act_t.at[0], act_t.at[1], pair_s.at[0], pair_r.at[0], partner)]
    swap[0].start()

    other_main = big.at[1, 1]

    def borders(df):
        f = slice(2 * df, 2 * df + 2)
        for copy in halo[:NOW] if df == 0 else halo[NOW:]:
            copy.wait_recv()

        @pl.when(row == 0)
        def _():
            main[f, 0] = jnp.zeros((2, COLS, C), BF16)
            cols[0, df, :, 0] = jnp.zeros((2, 16, C), BF16)

        @pl.when(row == 15)
        def _():
            main[f, ROWS + 1] = jnp.zeros((2, COLS, C), BF16)
            cols[0, df, :, 2] = jnp.zeros((2, 16, C), BF16)

        if df == 1:
            @pl.when(tm == 7)
            def _():
                main[f] = jnp.zeros((2, ROWS + 2, COLS, C), BF16)
                cols[0, df] = jnp.zeros((2, 3, 16, C), BF16)

        @pl.when(col == 0)
        def _():
            cols[0, df, 0] = jnp.zeros((3, 16, C), BF16)

        @pl.when(col == 3)
        def _():
            cols[0, df, 1] = jnp.zeros((3, 16, C), BF16)

        for copy in [
            remote(main.at[f], other_main.at[f], pair_s.at[1 + 2 * df], pair_r.at[1 + 2 * df], partner),
            remote(cols.at[0, df], cols.at[1, df], pair_s.at[2 + 2 * df], pair_r.at[2 + 2 * df], partner),
        ]:
            copy.start()
            swap.append(copy)
        for copy in swap:
            copy.wait()
        swap.clear()
        main[f, (ROWS + 1) * other] = big[1, 1, f, 1 + (ROWS - 1) * core]
        other_main[f, (ROWS + 1) * core] = main[f, ROWS - (ROWS - 1) * core]
        cols[0, df, :, 2 * other] = cols[1, df, :, 1]
        cols[1, df, :, 2 * core] = cols[0, df, :, 1]

    spot = lax.broadcasted_iota(jnp.int32, (COLS, C), 0)

    def shift(tile, df):
        edges = [[cols[tile, df, s, k].astype(F32) for k in range(3)] for s in (0, 1)]
        for f in (2 * df, 2 * df + 1):
            for r in range(ROWS + 2):
                k = 0 if r == 0 else 2 if r == ROWS + 1 else 1
                i = (f % 2) * ROWS + (r - 1) % ROWS
                value = big[tile, 1, f, r].astype(F32)
                after = jnp.where(spot == COLS - 1, edges[1][k][i : i + 1], pltpu.roll(value, COLS - 1, 0))
                before = jnp.where(spot == 0, edges[0][k][i : i + 1], pltpu.roll(value, 1, 0))
                big[tile, 0, f, r] = after.astype(BF16)
                big[tile, 2, f, r] = before.astype(BF16)

    def tap_grad(tap, at):
        a, b, c = tap // 9, (tap // 3) % 3, tap % 3
        total = jnp.zeros((C, C), F32)
        for tile in (0, 1):
            patch = big[tile, c, pl.ds(2 - a, 2), pl.ds(2 - b, ROWS)].reshape(CELLS, C)
            total += jnp.dot(act_t[tile], patch, preferred_element_type=F32)
        at = pl.multiple_of(at, 8)
        wgl_a[pl.ds(at, C), :] = total[:, 0:128]
        wgl_b[pl.ds(at, C), 0:64] = total[:, 128:C]

    lane = lax.broadcasted_iota(jnp.int32, (40, 128), 1)
    line = lax.broadcasted_iota(jnp.int32, (88, 128), 0)

    def pack(at):
        upper = jnp.where(
            line < SHARD, wgl_a[at : at + 88], jnp.where(line == SHARD, wgl_b[at + 80 : at + 81], 0.0)
        )
        lower = jnp.where(lane < 64, wgl_b[at : at + 40], pltpu.roll(wgl_b[at + 40 : at + 80], 64, 1))
        return jnp.concatenate([upper, lower], axis=0).astype(BF16)

    def e_copy(step):
        return remote(
            esend.at[(x + step) % 4], erecv.at[step - 1], e_s.at[step - 1], e_r.at[step - 1], x_dev(step)
        )

    borders(0)
    shift(0, 0)
    shift(1, 0)
    base = LATE * C + 24
    for i in range(EARLY):
        tap_grad(23 - 3 * core + i, base + i * C + 72 * core)
    for j in range(8):
        value = pack(base + 120 + SHARD * j)
        at = 64 * (j % 4) + 32 * (j // 4)
        for k in range(4):
            esend[k, at : at + 32] = value[32 * k : 32 * k + 32]
    for step in (1, 2, 3):
        e_copy(step).start()

    borders(1)
    shift(0, 1)
    shift(1, 1)
    for i in range(LATE):
        tap_grad(10 * core + i, i * C + 24 * other)
    for j in range(24):
        value = pack(24 + SHARD * j)
        if j % 4 == 3:
            fsend[j // 4] = value
        else:
            for k in range(4):
                xsend[k, j % 4, 32 * (j // 4) : 32 * (j // 4) + 32] = value[32 * k : 32 * k + 32]

    def y_row(k):
        return k + 6 * core if k < 6 else k + 8 - 2 * core

    def f_copy(k):
        return remote(fsend.at[k], frecv.at[y], f_s.at[k], f_r.at[y], (tm, y_row(k), col))

    for k in range(6):
        @pl.when(row != y_row(k))
        def _():
            f_copy(k).start()

        @pl.when(row == y_row(k))
        def _():
            frecv[y] = fsend[k]

    def h_copy(step):
        return remote(
            hsend.at[(x + step) % 4], hrecv.at[step - 1], h_s.at[step - 1], h_r.at[step - 1], x_dev(step)
        )

    def from_y(k):
        return jnp.logical_not(jnp.logical_and(self_y, y == k))

    def f_over_x():
        @pl.when(row < 12)
        def _():
            for k in range(8):
                @pl.when(from_y(k))
                def _():
                    remote(fsend.at[0], frecv.at[k], f_s.at[0], f_r.at[k], partner).wait_recv()

            total = frecv[0].astype(F32)
            for k in range(1, 8):
                total += frecv[k].astype(F32)
            htotal[...] = total.reshape(4, 32, 128)
            hsend[...] = total.astype(BF16).reshape(4, 32, 128)
            for step in (1, 2, 3):
                h_copy(step).start()

    def x_copy(w, step):
        return remote(
            xsend.at[(x + step) % 4, w], xrecv.at[step - 1, w],
            x_s.at[w, step - 1], x_r.at[w, step - 1], x_dev(step),
        )

    def x_start(w):
        for step in (1, 2, 3):
            x_copy(w, step).start()

    x_start(0)
    x_start(1)

    loads[2].wait()
    dact = jnp.zeros((CELLS, C), F32)
    for tap in range(27):
        a, b, c = tap // 9, (tap // 3) % 3, tap % 3
        patch = big[0, c, 2 - a : 4 - a, 2 - b : 2 - b + ROWS].reshape(CELLS, C)
        dact += jnp.dot(patch, w_v[:, tap * C : (tap + 1) * C], preferred_element_type=F32)
    inverse, normed, pre = norm()
    sigma = jax.nn.sigmoid(pre)
    dpre = dact * sigma * (1.0 + pre * (1.0 - sigma))
    gain_part = jnp.sum(dpre * normed, axis=0, keepdims=True)
    dnormed = dpre * gain[...]
    project = jnp.mean(dnormed * normed, axis=-1, keepdims=True)
    grad = cot[...].astype(F32).reshape(CELLS, C) + inverse * (dnormed - normed * project)
    fg_out[...] = grad.astype(BF16).reshape(2, ROWS, COLS, C)

    act32[0:8, :] = jnp.zeros((8, 256), F32)
    act32[0:1, :C] = gain_part
    gpart[0] = act32[0:8, 0:128]
    gpart[0, 1:2] = act32[0:1, 128:256]
    gain_steps = [
        [remote(gpart.at[0], grecv_x.at[0], g_s.at[0], g_r.at[0], partner)],
        [remote(gpart.at[1], grecv_x.at[k], g_s.at[k], g_r.at[k], x_dev(k)) for k in range(1, 4)],
        [remote(gpart.at[2], grecv_y.at[k - 1], g_s.at[3 + k], g_r.at[3 + k], y_dev(k)) for k in range(1, 8)],
        [remote(gpart.at[3], grecv_z.at[k - 1], g_s.at[10 + k], g_r.at[10 + k], z_dev(k)) for k in range(1, 8)],
    ]

    def gain_begin(n):
        for copy in gain_steps[n]:
            copy.start()

    def gain_end(n):
        for copy in gain_steps[n]:
            copy.wait()
        total = gpart[n]
        arrived = [grecv_x[0:1], grecv_x[1:4], grecv_y[...], grecv_z[...]][n]
        for k in range(len(gain_steps[n])):
            total += arrived[k]
        gpart[n + 1] = total

    gain_begin(0)

    def y_copy(w, k):
        return remote(
            ysend.at[w, 32 * k : 32 * k + 32], yrecv.at[w, y], y_s.at[w, k], y_r.at[w, y],
            (tm, y_row(k), col),
        )

    def z_copy(w, k):
        return remote(
            zsend.at[w, 16 * k : 16 * k + 16], zrecv.at[z], z_s.at[w, k], z_r.at[z], (2 * x + k, row, w)
        )

    def over_y(w):
        part = slice(64 * w, 64 * w + 64)
        extra = esend[x, part].astype(F32)
        for step in (1, 2, 3):
            extra += erecv[step - 1, part].astype(F32)
        ysend[w, 192:256] = extra.astype(BF16)
        if w < 3:
            for step in (1, 2, 3):
                x_copy(w, step).wait()
            if w == 0:
                x_start(2)
            value = xsend[x, w].astype(F32)
            for step in (1, 2, 3):
                value += xrecv[step - 1, w].astype(F32)
            ysend[w, 0:192] = value.astype(BF16)
        for k in range(8) if w < 3 else (6, 7):
            @pl.when(row != y_row(k))
            def _():
                y_copy(w, k).start()

            @pl.when(row == y_row(k))
            def _():
                yrecv[w, y] = ysend[w, 32 * k : 32 * k + 32]

    def y_sum(w):
        for k in range(8):
            @pl.when(from_y(k))
            def _():
                remote(ysend.at[w, 0:32], yrecv.at[w, k], y_s.at[w, 0], y_r.at[w, k], partner).wait_recv()

        total = yrecv[w, 0].astype(F32)
        for k in range(1, 8):
            total += yrecv[w, k].astype(F32)
        zsend[w] = total

    def over_z(w):
        if w < 3:
            y_sum(w)
        else:
            @pl.when(row < 12)
            def _():
                for step in (1, 2, 3):
                    h_copy(step).wait()
                total = htotal[x]
                for step in (1, 2, 3):
                    total += hrecv[step - 1].astype(F32)
                zsend[w] = total

            @pl.when(row >= 12)
            def _():
                y_sum(w)

        for k in range(2):
            @pl.when(z != 2 * w + k)
            def _():
                z_copy(w, k).start()

            @pl.when(z == 2 * w + k)
            def _():
                zrecv[z] = zsend[w, 16 * k : 16 * k + 16]

    for step in (1, 2, 3):
        e_copy(step).wait()
    over_y(3)
    over_y(0)
    gain_end(0)
    gain_begin(1)
    over_y(1)
    f_over_x()
    over_z(0)
    gain_end(1)
    gain_begin(2)
    over_y(2)
    over_z(3)
    over_z(1)
    gain_end(2)
    gain_begin(3)
    over_z(2)
    gain_end(3)

    for k in range(8):
        @pl.when(z != k)
        def _():
            remote(zsend.at[0, 0:16], zrecv.at[k], z_s.at[0, 0], z_r.at[k], partner).wait_recv()

    total = zrecv[0]
    for k in range(1, 8):
        total += zrecv[k]
    fin[tm] = total

    last = []
    for step in range(1, 8):
        last.append(remote(fin.at[tm], fin.at[tm], b_s.at[step - 1], b_r.at[step - 1], b_dev(step)))
        last[-1].start()
    for copy in last:
        copy.wait()

    scale = 1.0 / math.sqrt(16 * 96 * 128)
    gain_total = gpart[4] * scale
    gg_out[...] = jnp.concatenate([gain_total[0:1], gain_total[1:2]], axis=1)
    value = fin[...].reshape(128, 128) * scale
    wg_out[:, 0:128] = value[0:SHARD]
    wg_out[0:40, 128:C] = value[88:128, 0:64]
    wg_out[40:80, 128:C] = pltpu.roll(value[88:128], 64, 1)[:, 0:64]
    wg_out[80:81, 128:C] = value[81:82, 0:64]

    for copy in halo:
        copy.wait_send()
    for k in range(6):
        @pl.when(row != y_row(k))
        def _():
            f_copy(k).wait_send()

    for w in range(4):
        for k in range(8) if w < 3 else (6, 7):
            @pl.when(row != y_row(k))
            def _():
                y_copy(w, k).wait_send()

        for k in range(2):
            @pl.when(z != 2 * w + k)
            def _():
                z_copy(w, k).wait_send()


def per_device(features, cotangent, kernel, gain):
    vmem = pl.BlockSpec(memory_space=pltpu.VMEM)
    hbm = pl.BlockSpec(memory_space=pltpu.HBM)
    dma = pltpu.SemaphoreType.DMA
    fg, wg, gg = pl.pallas_call(
        body,
        out_shape=(
            jax.ShapeDtypeStruct((2, ROWS, COLS, C), BF16),
            jax.ShapeDtypeStruct((SHARD, C), F32),
            jax.ShapeDtypeStruct((1, 256), F32),
        ),
        in_specs=[hbm, hbm, hbm, vmem],
        out_specs=(vmem, vmem, vmem),
        scratch_shapes=[
            pltpu.VMEM((2, ROWS, COLS, C), BF16),
            pltpu.VMEM((2, ROWS, COLS, C), BF16),
            pltpu.VMEM((C, 27 * C), BF16),
            pltpu.VMEM((2, 3, 4, ROWS + 2, COLS, C), BF16),
            pltpu.VMEM((2, 2, 2, 3, 16, C), BF16),
            pltpu.VMEM((2, C, CELLS), BF16),
            pltpu.VMEM((2, 16, C), BF16),
            pltpu.VMEM((2, 16, C), F32),
            pltpu.VMEM((CELLS, 256), F32),
            pltpu.VMEM(((LATE + EARLY) * C + 96, 128), F32),
            pltpu.VMEM(((LATE + EARLY) * C + 96, 128), F32),
            pltpu.VMEM((4, 3, 192, 128), BF16),
            pltpu.VMEM((3, 3, 192, 128), BF16),
            pltpu.VMEM((4, 256, 128), BF16),
            pltpu.VMEM((3, 256, 128), BF16),
            pltpu.VMEM((6, 128, 128), BF16),
            pltpu.VMEM((8, 128, 128), BF16),
            pltpu.VMEM((4, 32, 128), F32),
            pltpu.VMEM((4, 32, 128), BF16),
            pltpu.VMEM((3, 32, 128), BF16),
            pltpu.VMEM((5, 8, 128), F32),
            pltpu.VMEM((4, 8, 128), F32),
            pltpu.VMEM((7, 8, 128), F32),
            pltpu.VMEM((7, 8, 128), F32),
            pltpu.VMEM((4, 256, 128), BF16),
            pltpu.VMEM((4, 8, 32, 128), BF16),
            pltpu.VMEM((4, 32, 128), F32),
            pltpu.VMEM((8, 16, 128), F32),
            pltpu.VMEM((8, 16, 128), F32),
            dma((3,)),
            dma((len(HALO),)), dma((len(HALO),)), dma((5,)), dma((5,)),
            dma((3, 3)), dma((3, 3)), dma((3,)), dma((3,)), dma((6,)), dma((8,)), dma((3,)), dma((3,)), dma((18,)), dma((18,)),
            dma((4, 8)), dma((4, 8)), dma((4, 2)), dma((8,)), dma((7,)), dma((7,)),
        ],
        compiler_params=pltpu.CompilerParams(
            collective_id=0, has_side_effects=True, vmem_limit_bytes=54912 * 1024
        ),
    )(features, cotangent, kernel.T, gain.reshape(1, C))
    return fg, wg, gg[0, :C]


def solution(mesh):
    return jax.shard_map(
        per_device,
        mesh=mesh,
        in_specs=(P("tm", "row", "col", None), P("tm", "row", "col", None), P(), P()),
        out_specs=(P("tm", "row", "col", None), P(("row", "col"), None), P()),
        check_vma=False,
    )
```

```python
import math

import jax
import jax.numpy as jnp
from jax import lax
from jax.experimental import pallas as pl
from jax.experimental.pallas import tpu as pltpu
from jax.sharding import PartitionSpec as P

MESH = pl.DeviceIdType.MESH
F32 = jnp.float32
BF16 = jnp.bfloat16
C = 192
ROWS, COLS = 6, 32
CELLS = 2 * ROWS * COLS
LATE, EARLY = 11, 4
SHARD = 81

HALO = [(0, 1, 0)] + [(0, out, dc) for out in (0, 1) for dc in (-1, 1)]
HALO += [(1, 0, 0), (1, 1, 0)] + [(1, out, dc) for out in (0, 1) for dc in (-1, 1)]
NOW = 5


def body(
    feat_hbm, cot_hbm, w_hbm, gain, fg_out, wg_out, gg_out,
    feat, cot, w_v, big, cols, act_t, packs, rows16, act32, wgl_a, wgl_b, xsend, xrecv, esend, erecv, fsend, frecv, htotal, hsend, hrecv,
    gpart, grecv, ysend, yrecv, zsend, zrecv, fin,
    in_sem, halo_s, halo_r, pair_s, pair_r, x_s, x_r, e_s, e_r, f_s, f_r, h_s, h_r, g_s, g_r, y_s, y_r, z_s, z_r, b_s, b_r,
):
    tm, row, col = lax.axis_index("tm"), lax.axis_index("row"), lax.axis_index("col")
    x, zlo = tm // 2, tm % 2
    y, core = row // 2, row % 2
    z = col * 2 + zlo
    other = 1 - core
    outward = 2 * core - 1
    partner = (tm, 2 * y + other, col)

    def near(dt, dr, dc):
        return ((tm + dt + 8) % 8, (row + dr + 16) % 16, (col + dc + 4) % 4)

    def x_dev(step):
        return (((x + step) % 4) * 2 + zlo, row, col)

    def z_dev(step):
        to = (z + step) % 8
        return (2 * x + to % 2, row, to // 2)

    def b_dev(step):
        return ((tm + step) % 8, row, col)

    def remote(src, dst, send, recv, device):
        return pltpu.make_async_remote_copy(
            src_ref=src, dst_ref=dst, send_sem=send, recv_sem=recv, device_id=device, device_id_type=MESH
        )

    main = big.at[0, 1]
    loads = [
        pltpu.make_async_copy(cot_hbm, cot, in_sem.at[0]),
        pltpu.make_async_copy(feat_hbm, feat, in_sem.at[1]),
        pltpu.make_async_copy(w_hbm, w_v, in_sem.at[2]),
    ]
    for copy in loads:
        copy.start()

    barrier = pltpu.get_barrier_semaphore()

    def greet(device):
        pl.semaphore_signal(barrier, inc=1, device_id=device, device_id_type=MESH)

    for df, out, dc in HALO:
        greet(near(df, outward * out, -dc))
    greet(partner)
    for step in range(1, 4):
        greet(x_dev(4 - step))
    for step in range(1, 8):
        greet(z_dev(8 - step))
        greet(b_dev(8 - step))
    holder = jnp.logical_and(row >= 6, row < 14).astype(jnp.int32)
    self_y = core == holder
    for k in range(8):
        @pl.when(jnp.logical_not(jnp.logical_and(self_y, y == k)))
        def _():
            greet((tm, 2 * k + holder, col))

    loads[0].wait()
    for side, q in ((0, 0), (1, COLS - 1)):
        rows16[side] = jnp.zeros((16, C), F32)
        for f in range(2):
            for r in range(ROWS):
                i = f * ROWS + r
                rows16[side, i : i + 1, :] = cot[f, r].astype(F32)[q : q + 1, :]
        packs[side] = rows16[side].astype(BF16)

    expected = len(HALO) + 1 + 3 + 7 + 7 + 8
    pl.semaphore_wait(barrier, expected - self_y.astype(jnp.int32))

    halo = []
    for m, (df, out, dc) in enumerate(HALO):
        if dc != 0:
            src = packs.at[0 if dc < 0 else 1]
            dst = cols.at[0, df, 1 if dc < 0 else 0, 2 * other if out else 1]
        elif out:
            src, dst = cot.at[:, (ROWS - 1) * core], main.at[2 * df : 2 * df + 2, (ROWS + 1) * other]
        else:
            src, dst = cot, main.at[2:4, 1 : ROWS + 1]
        halo.append(remote(src, dst, halo_s.at[m], halo_r.at[m], near(-df, outward * out, dc)))
        halo[-1].start()
    main[0:2, 1 : ROWS + 1] = cot[...]

    def norm():
        wide = feat[...].astype(F32).reshape(CELLS, C)
        inverse = lax.rsqrt(jnp.mean(wide * wide, axis=-1, keepdims=True) + 1e-06)
        normed = wide * inverse
        return inverse, normed, normed * gain[...]

    loads[1].wait()
    pre = norm()[2]
    act32[:, C:] = jnp.zeros((CELLS, 256 - C), F32)
    act32[:, :C] = pre * jax.nn.sigmoid(pre)
    act_t[0] = act32[...].T[:C].astype(BF16)
    swap = [remote(act_t.at[0], act_t.at[1], pair_s.at[0], pair_r.at[0], partner)]
    swap[0].start()

    other_main = big.at[1, 1]

    def borders(df):
        f = slice(2 * df, 2 * df + 2)
        for copy in halo[:NOW] if df == 0 else halo[NOW:]:
            copy.wait_recv()

        @pl.when(row == 0)
        def _():
            main[f, 0] = jnp.zeros((2, COLS, C), BF16)
            cols[0, df, :, 0] = jnp.zeros((2, 16, C), BF16)

        @pl.when(row == 15)
        def _():
            main[f, ROWS + 1] = jnp.zeros((2, COLS, C), BF16)
            cols[0, df, :, 2] = jnp.zeros((2, 16, C), BF16)

        if df == 1:
            @pl.when(tm == 7)
            def _():
                main[f] = jnp.zeros((2, ROWS + 2, COLS, C), BF16)
                cols[0, df] = jnp.zeros((2, 3, 16, C), BF16)

        @pl.when(col == 0)
        def _():
            cols[0, df, 0] = jnp.zeros((3, 16, C), BF16)

        @pl.when(col == 3)
        def _():
            cols[0, df, 1] = jnp.zeros((3, 16, C), BF16)

        for copy in [
            remote(main.at[f], other_main.at[f], pair_s.at[1 + 2 * df], pair_r.at[1 + 2 * df], partner),
            remote(cols.at[0, df], cols.at[1, df], pair_s.at[2 + 2 * df], pair_r.at[2 + 2 * df], partner),
        ]:
            copy.start()
            swap.append(copy)
        for copy in swap:
            copy.wait()
        swap.clear()
        main[f, (ROWS + 1) * other] = big[1, 1, f, 1 + (ROWS - 1) * core]
        other_main[f, (ROWS + 1) * core] = main[f, ROWS - (ROWS - 1) * core]
        cols[0, df, :, 2 * other] = cols[1, df, :, 1]
        cols[1, df, :, 2 * core] = cols[0, df, :, 1]

    spot = lax.broadcasted_iota(jnp.int32, (COLS, C), 0)

    def shift(tile, df):
        edges = [[cols[tile, df, s, k].astype(F32) for k in range(3)] for s in (0, 1)]
        for f in (2 * df, 2 * df + 1):
            for r in range(ROWS + 2):
                k = 0 if r == 0 else 2 if r == ROWS + 1 else 1
                i = (f % 2) * ROWS + (r - 1) % ROWS
                value = big[tile, 1, f, r].astype(F32)
                after = jnp.where(spot == COLS - 1, edges[1][k][i : i + 1], pltpu.roll(value, COLS - 1, 0))
                before = jnp.where(spot == 0, edges[0][k][i : i + 1], pltpu.roll(value, 1, 0))
                big[tile, 0, f, r] = after.astype(BF16)
                big[tile, 2, f, r] = before.astype(BF16)

    def tap_grad(tap, at):
        a, b, c = tap // 9, (tap // 3) % 3, tap % 3
        total = jnp.zeros((C, C), F32)
        for tile in (0, 1):
            patch = big[tile, c, pl.ds(2 - a, 2), pl.ds(2 - b, ROWS)].reshape(CELLS, C)
            total += jnp.dot(act_t[tile], patch, preferred_element_type=F32)
        at = pl.multiple_of(at, 8)
        wgl_a[pl.ds(at, C), :] = total[:, 0:128]
        wgl_b[pl.ds(at, C), 0:64] = total[:, 128:C]

    lane = lax.broadcasted_iota(jnp.int32, (40, 128), 1)
    line = lax.broadcasted_iota(jnp.int32, (88, 128), 0)

    def pack(at):
        upper = jnp.where(
            line < SHARD, wgl_a[at : at + 88], jnp.where(line == SHARD, wgl_b[at + 80 : at + 81], 0.0)
        )
        lower = jnp.where(lane < 64, wgl_b[at : at + 40], pltpu.roll(wgl_b[at + 40 : at + 80], 64, 1))
        return jnp.concatenate([upper, lower], axis=0).astype(BF16)

    def e_copy(step):
        return remote(
            esend.at[(x + step) % 4], erecv.at[step - 1], e_s.at[step - 1], e_r.at[step - 1], x_dev(step)
        )

    borders(0)
    shift(0, 0)
    shift(1, 0)
    base = LATE * C + 24
    for i in range(EARLY):
        tap_grad(23 - 3 * core + i, base + i * C + 72 * core)
    for j in range(8):
        value = pack(base + 120 + SHARD * j)
        at = 64 * (j % 4) + 32 * (j // 4)
        for k in range(4):
            esend[k, at : at + 32] = value[32 * k : 32 * k + 32]
    for step in (1, 2, 3):
        e_copy(step).start()

    borders(1)
    shift(0, 1)
    shift(1, 1)
    for i in range(LATE):
        tap_grad(10 * core + i, i * C + 24 * other)
    for j in range(24):
        value = pack(24 + SHARD * j)
        if j % 4 == 3:
            fsend[j // 4] = value
        else:
            for k in range(4):
                xsend[k, j % 4, 32 * (j // 4) : 32 * (j // 4) + 32] = value[32 * k : 32 * k + 32]

    def y_row(k):
        return k + 6 * core if k < 6 else k + 8 - 2 * core

    def f_copy(k):
        return remote(fsend.at[k], frecv.at[y], f_s.at[k], f_r.at[y], (tm, y_row(k), col))

    for k in range(6):
        @pl.when(row != y_row(k))
        def _():
            f_copy(k).start()

        @pl.when(row == y_row(k))
        def _():
            frecv[y] = fsend[k]

    def h_copy(step):
        return remote(
            hsend.at[(x + step) % 4], hrecv.at[step - 1], h_s.at[step - 1], h_r.at[step - 1], x_dev(step)
        )

    def from_y(k):
        return jnp.logical_not(jnp.logical_and(self_y, y == k))

    def f_over_x():
        @pl.when(row < 12)
        def _():
            for k in range(8):
                @pl.when(from_y(k))
                def _():
                    remote(fsend.at[0], frecv.at[k], f_s.at[0], f_r.at[k], partner).wait_recv()

            total = frecv[0].astype(F32)
            for k in range(1, 8):
                total += frecv[k].astype(F32)
            htotal[...] = total.reshape(4, 32, 128)
            hsend[...] = total.astype(BF16).reshape(4, 32, 128)
            for step in (1, 2, 3):
                h_copy(step).start()

    def x_copy(w, step):
        return remote(
            xsend.at[(x + step) % 4, w], xrecv.at[step - 1, w],
            x_s.at[w, step - 1], x_r.at[w, step - 1], x_dev(step),
        )

    def x_start(w):
        for step in (1, 2, 3):
            x_copy(w, step).start()

    x_start(0)
    x_start(1)

    loads[2].wait()
    dact = jnp.zeros((CELLS, C), F32)
    for tap in range(27):
        a, b, c = tap // 9, (tap // 3) % 3, tap % 3
        patch = big[0, c, 2 - a : 4 - a, 2 - b : 2 - b + ROWS].reshape(CELLS, C)
        dact += jnp.dot(patch, w_v[:, tap * C : (tap + 1) * C], preferred_element_type=F32)
    inverse, normed, pre = norm()
    sigma = jax.nn.sigmoid(pre)
    dpre = dact * sigma * (1.0 + pre * (1.0 - sigma))
    gain_part = jnp.sum(dpre * normed, axis=0, keepdims=True)
    dnormed = dpre * gain[...]
    project = jnp.mean(dnormed * normed, axis=-1, keepdims=True)
    grad = cot[...].astype(F32).reshape(CELLS, C) + inverse * (dnormed - normed * project)
    fg_out[...] = grad.astype(BF16).reshape(2, ROWS, COLS, C)

    act32[0:8, :] = jnp.zeros((8, 256), F32)
    act32[0:1, :C] = gain_part
    gpart[0] = act32[0:8, 0:128]
    gpart[0, 1:2] = act32[0:1, 128:256]
    gain_pair = remote(gpart.at[0], grecv.at[0], g_s.at[0], g_r.at[0], partner)
    gain_pair.start()
    gain_cols = [
        remote(gpart.at[1], grecv.at[k], g_s.at[k], g_r.at[k], (tm, row, (col + k) % 4)) for k in (1, 2, 3)
    ]

    def y_part(w):
        return slice(0, 48 if w == 0 else 32)

    def y_copy(w, k):
        return remote(
            ysend.at[w, k, y_part(w)], yrecv.at[w, y, y_part(w)], y_s.at[w, k], y_r.at[w, y],
            (tm, y_row(k), col),
        )

    def z_copy(w, k):
        return remote(
            zsend.at[w, 16 * k : 16 * k + 16], zrecv.at[z], z_s.at[w, k], z_r.at[z], (2 * x + k, row, w)
        )

    def over_y(w):
        part = slice(64 * w, 64 * w + 64)
        extra = esend[x, part].astype(F32)
        for step in (1, 2, 3):
            extra += erecv[step - 1, part].astype(F32)
        ysend[w, 6:8, 0:32] = extra.astype(BF16).reshape(2, 32, 128)
        if w < 3:
            for step in (1, 2, 3):
                x_copy(w, step).wait()
            if w == 0:
                x_start(2)
            value = xsend[x, w].astype(F32)
            for step in (1, 2, 3):
                value += xrecv[step - 1, w].astype(F32)
            ysend[w, 0:6, 0:32] = value.astype(BF16).reshape(6, 32, 128)
        if w == 0:
            gain_pair.wait()
            total = gpart[0] + grecv[0]
            upper = total.astype(BF16).astype(F32)
            both = jnp.concatenate([upper, total - upper], axis=0).astype(BF16)
            for k in range(8):
                ysend[w, k, 32:48] = both
        for k in range(8) if w < 3 else (6, 7):
            @pl.when(row != y_row(k))
            def _():
                y_copy(w, k).start()

            @pl.when(row == y_row(k))
            def _():
                yrecv[w, y, y_part(w)] = ysend[w, k, y_part(w)]

    def y_sum(w):
        for k in range(8):
            @pl.when(from_y(k))
            def _():
                remote(
                    ysend.at[w, 0, y_part(w)], yrecv.at[w, k, y_part(w)], y_s.at[w, 0], y_r.at[w, k], partner
                ).wait_recv()

        total = yrecv[w, 0, y_part(w)].astype(F32)
        for k in range(1, 8):
            total += yrecv[w, k, y_part(w)].astype(F32)
        zsend[w] = total[0:32]
        if w == 0:
            gpart[1] = total[32:40] + total[40:48]

    def over_z(w):
        if w < 3:
            y_sum(w)
        else:
            @pl.when(row < 12)
            def _():
                for step in (1, 2, 3):
                    h_copy(step).wait()
                total = htotal[x]
                for step in (1, 2, 3):
                    total += hrecv[step - 1].astype(F32)
                zsend[w] = total

            @pl.when(row >= 12)
            def _():
                y_sum(w)

        for k in range(2):
            @pl.when(z != 2 * w + k)
            def _():
                z_copy(w, k).start()

            @pl.when(z == 2 * w + k)
            def _():
                zrecv[z] = zsend[w, 16 * k : 16 * k + 16]

    for step in (1, 2, 3):
        e_copy(step).wait()
    over_y(3)
    over_y(0)
    over_y(1)
    f_over_x()
    over_y(2)
    over_z(0)
    for copy in gain_cols:
        copy.start()
    over_z(3)
    over_z(1)
    over_z(2)

    for k in range(8):
        @pl.when(z != k)
        def _():
            remote(zsend.at[0, 0:16], zrecv.at[k], z_s.at[0, 0], z_r.at[k], partner).wait_recv()

    total = zrecv[0]
    for k in range(1, 8):
        total += zrecv[k]
    fin[tm, 0:16] = total
    for copy in gain_cols:
        copy.wait()
    fin[tm, 16:24] = gpart[1] + grecv[1] + grecv[2] + grecv[3]

    last = []
    for step in range(1, 8):
        last.append(remote(fin.at[tm], fin.at[tm], b_s.at[step - 1], b_r.at[step - 1], b_dev(step)))
        last[-1].start()

    for copy in halo:
        copy.wait_send()
    for k in range(6):
        @pl.when(row != y_row(k))
        def _():
            f_copy(k).wait_send()

    for w in range(4):
        for k in range(8) if w < 3 else (6, 7):
            @pl.when(row != y_row(k))
            def _():
                y_copy(w, k).wait_send()

        for k in range(2):
            @pl.when(z != 2 * w + k)
            def _():
                z_copy(w, k).wait_send()

    for copy in last:
        copy.wait()
    scale = 1.0 / math.sqrt(16 * 96 * 128)
    gain_total = fin[0, 16:24]
    for k in range(1, 8):
        gain_total += fin[k, 16:24]
    gain_total *= scale
    gg_out[...] = jnp.concatenate([gain_total[0:1], gain_total[1:2]], axis=1)
    value = fin[:, 0:16].reshape(128, 128) * scale
    wg_out[:, 0:128] = value[0:SHARD]
    wg_out[0:40, 128:C] = value[88:128, 0:64]
    wg_out[40:80, 128:C] = pltpu.roll(value[88:128], 64, 1)[:, 0:64]
    wg_out[80:81, 128:C] = value[81:82, 0:64]


def per_device(features, cotangent, kernel, gain):
    vmem = pl.BlockSpec(memory_space=pltpu.VMEM)
    hbm = pl.BlockSpec(memory_space=pltpu.HBM)
    dma = pltpu.SemaphoreType.DMA
    fg, wg, gg = pl.pallas_call(
        body,
        out_shape=(
            jax.ShapeDtypeStruct((2, ROWS, COLS, C), BF16),
            jax.ShapeDtypeStruct((SHARD, C), F32),
            jax.ShapeDtypeStruct((1, 256), F32),
        ),
        in_specs=[hbm, hbm, hbm, vmem],
        out_specs=(vmem, vmem, vmem),
        scratch_shapes=[
            pltpu.VMEM((2, ROWS, COLS, C), BF16),
            pltpu.VMEM((2, ROWS, COLS, C), BF16),
            pltpu.VMEM((C, 27 * C), BF16),
            pltpu.VMEM((2, 3, 4, ROWS + 2, COLS, C), BF16),
            pltpu.VMEM((2, 2, 2, 3, 16, C), BF16),
            pltpu.VMEM((2, C, CELLS), BF16),
            pltpu.VMEM((2, 16, C), BF16),
            pltpu.VMEM((2, 16, C), F32),
            pltpu.VMEM((CELLS, 256), F32),
            pltpu.VMEM(((LATE + EARLY) * C + 96, 128), F32),
            pltpu.VMEM(((LATE + EARLY) * C + 96, 128), F32),
            pltpu.VMEM((4, 3, 192, 128), BF16),
            pltpu.VMEM((3, 3, 192, 128), BF16),
            pltpu.VMEM((4, 256, 128), BF16),
            pltpu.VMEM((3, 256, 128), BF16),
            pltpu.VMEM((6, 128, 128), BF16),
            pltpu.VMEM((8, 128, 128), BF16),
            pltpu.VMEM((4, 32, 128), F32),
            pltpu.VMEM((4, 32, 128), BF16),
            pltpu.VMEM((3, 32, 128), BF16),
            pltpu.VMEM((2, 8, 128), F32),
            pltpu.VMEM((4, 8, 128), F32),
            pltpu.VMEM((4, 8, 48, 128), BF16),
            pltpu.VMEM((4, 8, 48, 128), BF16),
            pltpu.VMEM((4, 32, 128), F32),
            pltpu.VMEM((8, 16, 128), F32),
            pltpu.VMEM((8, 24, 128), F32),
            dma((3,)),
            dma((len(HALO),)), dma((len(HALO),)), dma((5,)), dma((5,)),
            dma((3, 3)), dma((3, 3)), dma((3,)), dma((3,)), dma((6,)), dma((8,)), dma((3,)), dma((3,)), dma((4,)), dma((4,)),
            dma((4, 8)), dma((4, 8)), dma((4, 2)), dma((8,)), dma((7,)), dma((7,)),
        ],
        compiler_params=pltpu.CompilerParams(
            collective_id=0, has_side_effects=True, vmem_limit_bytes=54912 * 1024
        ),
    )(features, cotangent, kernel.T, gain.reshape(1, C))
    return fg, wg, gg[0, :C]


def solution(mesh):
    return jax.shard_map(
        per_device,
        mesh=mesh,
        in_specs=(P("tm", "row", "col", None), P("tm", "row", "col", None), P(), P()),
        out_specs=(P("tm", "row", "col", None), P(("row", "col"), None), P()),
        check_vma=False,
    )
```

```python
import math

import jax
import jax.numpy as jnp
from jax import lax
from jax.experimental import pallas as pl
from jax.experimental.pallas import tpu as pltpu
from jax.sharding import PartitionSpec as P

MESH = pl.DeviceIdType.MESH
F32 = jnp.float32
BF16 = jnp.bfloat16
C = 192
ROWS, COLS = 6, 32
CELLS = 2 * ROWS * COLS
LATE, EARLY = 11, 4
SHARD = 81

HALO = [(0, 1, 0)] + [(0, out, dc) for out in (0, 1) for dc in (-1, 1)]
HALO += [(1, 0, 0), (1, 1, 0)] + [(1, out, dc) for out in (0, 1) for dc in (-1, 1)]
NOW = 5


def body(
    feat_hbm, cot_hbm, w_hbm, gain, fg_out, wg_out, gg_out,
    feat, cot, w_v, big, cols, act_t, packs, rows16, act32, wgl_a, wgl_b, xsend, xrecv, esend, erecv, fsend, frecv, htotal, hsend, hrecv,
    gpart, grecv, ysend, yrecv, zsend, zrecv, fin,
    in_sem, halo_s, halo_r, tile_s, tile_r, pair_s, pair_r, x_s, x_r, e_s, e_r, f_s, f_r, h_s, h_r, g_s, g_r, y_s, y_r, z_s, z_r, b_s, b_r,
):
    tm, row, col = lax.axis_index("tm"), lax.axis_index("row"), lax.axis_index("col")
    x, zlo = tm // 2, tm % 2
    y, core = row // 2, row % 2
    z = col * 2 + zlo
    other = 1 - core
    outward = 2 * core - 1
    partner = (tm, 2 * y + other, col)

    def near(dt, dr, dc):
        return ((tm + dt + 8) % 8, (row + dr + 16) % 16, (col + dc + 4) % 4)

    def x_dev(step):
        return (((x + step) % 4) * 2 + zlo, row, col)

    def z_dev(step):
        to = (z + step) % 8
        return (2 * x + to % 2, row, to // 2)

    def b_dev(step):
        return ((tm + step) % 8, row, col)

    def remote(src, dst, send, recv, device):
        return pltpu.make_async_remote_copy(
            src_ref=src, dst_ref=dst, send_sem=send, recv_sem=recv, device_id=device, device_id_type=MESH
        )

    main = big.at[0, 1]
    loads = [
        pltpu.make_async_copy(cot_hbm, cot, in_sem.at[0]),
        pltpu.make_async_copy(feat_hbm, feat, in_sem.at[1]),
        pltpu.make_async_copy(w_hbm, w_v, in_sem.at[2]),
    ]
    for copy in loads:
        copy.start()

    barrier = pltpu.get_barrier_semaphore()

    def greet(device):
        pl.semaphore_signal(barrier, inc=1, device_id=device, device_id_type=MESH)

    for df, out, dc in HALO:
        greet(near(df, outward * out, -dc))
    greet(partner)
    for step in range(1, 4):
        greet(x_dev(4 - step))
    for step in range(1, 8):
        greet(z_dev(8 - step))
        greet(b_dev(8 - step))
    holder = jnp.logical_and(row >= 6, row < 14).astype(jnp.int32)
    self_y = core == holder
    for k in range(8):
        @pl.when(jnp.logical_not(jnp.logical_and(self_y, y == k)))
        def _():
            greet((tm, 2 * k + holder, col))

    loads[0].wait()
    for side, q in ((0, 0), (1, COLS - 1)):
        rows16[side] = jnp.zeros((16, C), F32)
        for f in range(2):
            for r in range(ROWS):
                i = f * ROWS + r
                rows16[side, i : i + 1, :] = cot[f, r].astype(F32)[q : q + 1, :]
        packs[side] = rows16[side].astype(BF16)

    expected = len(HALO) + 1 + 3 + 7 + 7 + 8
    pl.semaphore_wait(barrier, expected - self_y.astype(jnp.int32))

    halo, tile = [], []
    for m, (df, out, dc) in enumerate(HALO):
        if dc != 0:
            src = packs.at[0 if dc < 0 else 1]
            dst = cols.at[0, df, 1 if dc < 0 else 0, 2 * other if out else 1]
        elif out:
            src, dst = cot.at[:, (ROWS - 1) * core], main.at[2 * df : 2 * df + 2, (ROWS + 1) * other]
        else:
            for f in (0, 1):
                tile.append(remote(
                    cot.at[f], main.at[2 + f, 1 : ROWS + 1], tile_s.at[f], tile_r.at[f], near(-1, 0, 0)
                ))
                tile[-1].start()
            continue
        halo.append(remote(src, dst, halo_s.at[m], halo_r.at[m], near(-df, outward * out, dc)))
        halo[-1].start()

    other_main = big.at[1, 1]
    swap = []

    def hand_over(n, src, dst):
        swap.append(remote(src, dst, pair_s.at[n], pair_r.at[n], partner))
        swap[-1].start()

    hand_over(0, cot, other_main.at[0:2, 1 : ROWS + 1])
    main[0:2, 1 : ROWS + 1] = cot[...]

    def norm():
        wide = feat[...].astype(F32).reshape(CELLS, C)
        inverse = lax.rsqrt(jnp.mean(wide * wide, axis=-1, keepdims=True) + 1e-06)
        normed = wide * inverse
        return inverse, normed, normed * gain[...]

    loads[1].wait()
    pre = norm()[2]
    act32[:, C:] = jnp.zeros((CELLS, 256 - C), F32)
    act32[:, :C] = pre * jax.nn.sigmoid(pre)
    act_t[0] = act32[...].T[:C].astype(BF16)
    hand_over(1, act_t.at[0], act_t.at[1])

    def borders(df):
        f = slice(2 * df, 2 * df + 2)
        if df == 1:
            for n in (0, 1):
                tile[n].wait_recv()

                @pl.when(tm == 7)
                def _():
                    main[2 + n, 1 : ROWS + 1] = jnp.zeros((ROWS, COLS, C), BF16)

                inner = (2 + n, slice(1, ROWS + 1))
                hand_over(4 + n, main.at[inner], other_main.at[inner])
        for copy in halo[:NOW] if df == 0 else halo[NOW:]:
            copy.wait_recv()

        @pl.when(row == 0)
        def _():
            main[f, 0] = jnp.zeros((2, COLS, C), BF16)
            cols[0, df, :, 0] = jnp.zeros((2, 16, C), BF16)

        @pl.when(row == 15)
        def _():
            main[f, ROWS + 1] = jnp.zeros((2, COLS, C), BF16)
            cols[0, df, :, 2] = jnp.zeros((2, 16, C), BF16)

        if df == 1:
            @pl.when(tm == 7)
            def _():
                main[f, (ROWS + 1) * core] = jnp.zeros((2, COLS, C), BF16)
                cols[0, df] = jnp.zeros((2, 3, 16, C), BF16)

        @pl.when(col == 0)
        def _():
            cols[0, df, 0] = jnp.zeros((3, 16, C), BF16)

        @pl.when(col == 3)
        def _():
            cols[0, df, 1] = jnp.zeros((3, 16, C), BF16)

        edge = (ROWS + 1) * core
        hand_over(2 + 4 * df, main.at[f, edge], other_main.at[f, edge])
        hand_over(3 + 4 * df, cols.at[0, df], cols.at[1, df])
        for copy in swap:
            copy.wait()
        swap.clear()
        main[f, (ROWS + 1) * other] = big[1, 1, f, 1 + (ROWS - 1) * core]
        other_main[f, (ROWS + 1) * core] = main[f, ROWS - (ROWS - 1) * core]
        cols[0, df, :, 2 * other] = cols[1, df, :, 1]
        cols[1, df, :, 2 * core] = cols[0, df, :, 1]

    spot = lax.broadcasted_iota(jnp.int32, (COLS, C), 0)

    def shift(tile, df):
        edges = [[cols[tile, df, s, k].astype(F32) for k in range(3)] for s in (0, 1)]
        for f in (2 * df, 2 * df + 1):
            for r in range(ROWS + 2):
                k = 0 if r == 0 else 2 if r == ROWS + 1 else 1
                i = (f % 2) * ROWS + (r - 1) % ROWS
                value = big[tile, 1, f, r].astype(F32)
                after = jnp.where(spot == COLS - 1, edges[1][k][i : i + 1], pltpu.roll(value, COLS - 1, 0))
                before = jnp.where(spot == 0, edges[0][k][i : i + 1], pltpu.roll(value, 1, 0))
                big[tile, 0, f, r] = after.astype(BF16)
                big[tile, 2, f, r] = before.astype(BF16)

    def tap_grad(tap, at):
        a, b, c = tap // 9, (tap // 3) % 3, tap % 3
        total = jnp.zeros((C, C), F32)
        for tile in (0, 1):
            patch = big[tile, c, pl.ds(2 - a, 2), pl.ds(2 - b, ROWS)].reshape(CELLS, C)
            total += jnp.dot(act_t[tile], patch, preferred_element_type=F32)
        at = pl.multiple_of(at, 8)
        wgl_a[pl.ds(at, C), :] = total[:, 0:128]
        wgl_b[pl.ds(at, C), 0:64] = total[:, 128:C]

    lane = lax.broadcasted_iota(jnp.int32, (40, 128), 1)
    line = lax.broadcasted_iota(jnp.int32, (88, 128), 0)

    def pack(at):
        upper = jnp.where(
            line < SHARD, wgl_a[at : at + 88], jnp.where(line == SHARD, wgl_b[at + 80 : at + 81], 0.0)
        )
        lower = jnp.where(lane < 64, wgl_b[at : at + 40], pltpu.roll(wgl_b[at + 40 : at + 80], 64, 1))
        return jnp.concatenate([upper, lower], axis=0).astype(BF16)

    def e_copy(step):
        return remote(
            esend.at[(x + step) % 4], erecv.at[step - 1], e_s.at[step - 1], e_r.at[step - 1], x_dev(step)
        )

    def y_row(k):
        return k + 6 * core if k < 6 else k + 8 - 2 * core

    def f_copy(k):
        return remote(fsend.at[k], frecv.at[y], f_s.at[k], f_r.at[y], (tm, y_row(k), col))

    def f_start(chunks):
        for k in chunks:
            @pl.when(row != y_row(k))
            def _():
                f_copy(k).start()

            @pl.when(row == y_row(k))
            def _():
                frecv[y] = fsend[k]

    borders(0)
    shift(0, 0)
    shift(1, 0)
    base = LATE * C + 24
    for i in range(EARLY):
        tap_grad(23 - 3 * core + i, base + i * C + 72 * core)
    for j in range(8):
        value = pack(base + 120 + SHARD * j)
        at = 64 * (j % 4) + 32 * (j // 4)
        if j % 4 == 3:
            fsend[6 + j // 4] = value
        else:
            for k in range(4):
                esend[k, at : at + 32] = value[32 * k : 32 * k + 32]
    for step in (1, 2, 3):
        e_copy(step).start()
    f_start((6, 7))

    borders(1)
    shift(0, 1)
    shift(1, 1)
    for i in range(LATE):
        tap_grad(10 * core + i, i * C + 24 * other)
    for j in range(24):
        value = pack(24 + SHARD * j)
        if j % 4 == 3:
            fsend[j // 4] = value
        else:
            for k in range(4):
                xsend[k, j % 4, 32 * (j // 4) : 32 * (j // 4) + 32] = value[32 * k : 32 * k + 32]

    f_start(range(6))

    def h_copy(step):
        return remote(
            hsend.at[(x + step) % 4], hrecv.at[step - 1], h_s.at[step - 1], h_r.at[step - 1], x_dev(step)
        )

    def from_y(k):
        return jnp.logical_not(jnp.logical_and(self_y, y == k))

    def f_over_x():
        for k in range(8):
            @pl.when(from_y(k))
            def _():
                remote(fsend.at[0], frecv.at[k], f_s.at[0], f_r.at[k], partner).wait_recv()

        total = frecv[0].astype(F32)
        for k in range(1, 8):
            total += frecv[k].astype(F32)
        htotal[...] = total.reshape(4, 32, 128)
        hsend[...] = total.astype(BF16).reshape(4, 32, 128)
        for step in (1, 2, 3):
            h_copy(step).start()

    def x_copy(w, step):
        return remote(
            xsend.at[(x + step) % 4, w], xrecv.at[step - 1, w],
            x_s.at[w, step - 1], x_r.at[w, step - 1], x_dev(step),
        )

    def x_start(w):
        for step in (1, 2, 3):
            x_copy(w, step).start()

    x_start(0)
    x_start(1)

    loads[2].wait()
    dact = jnp.zeros((CELLS, C), F32)
    for tap in range(27):
        a, b, c = tap // 9, (tap // 3) % 3, tap % 3
        patch = big[0, c, 2 - a : 4 - a, 2 - b : 2 - b + ROWS].reshape(CELLS, C)
        dact += jnp.dot(patch, w_v[:, tap * C : (tap + 1) * C], preferred_element_type=F32)
    inverse, normed, pre = norm()
    sigma = jax.nn.sigmoid(pre)
    dpre = dact * sigma * (1.0 + pre * (1.0 - sigma))
    gain_part = jnp.sum(dpre * normed, axis=0, keepdims=True)
    dnormed = dpre * gain[...]
    project = jnp.mean(dnormed * normed, axis=-1, keepdims=True)
    grad = cot[...].astype(F32).reshape(CELLS, C) + inverse * (dnormed - normed * project)
    fg_out[...] = grad.astype(BF16).reshape(2, ROWS, COLS, C)

    act32[0:8, :] = jnp.zeros((8, 256), F32)
    act32[0:1, :C] = gain_part
    gpart[0] = act32[0:8, 0:128]
    gpart[0, 1:2] = act32[0:1, 128:256]
    gain_pair = remote(gpart.at[0], grecv.at[0], g_s.at[0], g_r.at[0], partner)
    gain_pair.start()
    gain_cols = [
        remote(gpart.at[1], grecv.at[k], g_s.at[k], g_r.at[k], (tm, row, (col + k) % 4)) for k in (1, 2, 3)
    ]

    def y_part(w):
        return slice(0, 48 if w == 0 else 32)

    def y_copy(w, k):
        return remote(
            ysend.at[w, k, y_part(w)], yrecv.at[w, y, y_part(w)], y_s.at[w, k], y_r.at[w, y],
            (tm, y_row(k), col),
        )

    def z_copy(w, k):
        return remote(
            zsend.at[w, 16 * k : 16 * k + 16], zrecv.at[z], z_s.at[w, k], z_r.at[z], (2 * x + k, row, w)
        )

    def over_y(w):
        part = slice(64 * w, 64 * w + 64)
        extra = esend[x, part].astype(F32)
        for step in (1, 2, 3):
            extra += erecv[step - 1, part].astype(F32)
        ysend[w, 6:8, 0:32] = extra.astype(BF16).reshape(2, 32, 128)
        for step in (1, 2, 3):
            x_copy(w, step).wait()
        if w == 0:
            x_start(2)
        value = xsend[x, w].astype(F32)
        for step in (1, 2, 3):
            value += xrecv[step - 1, w].astype(F32)
        ysend[w, 0:6, 0:32] = value.astype(BF16).reshape(6, 32, 128)
        if w == 0:
            gain_pair.wait()
            total = gpart[0] + grecv[0]
            upper = total.astype(BF16).astype(F32)
            both = jnp.concatenate([upper, total - upper], axis=0).astype(BF16)
            for k in range(8):
                ysend[w, k, 32:48] = both
        for k in range(8):
            @pl.when(row != y_row(k))
            def _():
                y_copy(w, k).start()

            @pl.when(row == y_row(k))
            def _():
                yrecv[w, y, y_part(w)] = ysend[w, k, y_part(w)]

    def y_sum(w):
        for k in range(8):
            @pl.when(from_y(k))
            def _():
                remote(
                    ysend.at[w, 0, y_part(w)], yrecv.at[w, k, y_part(w)], y_s.at[w, 0], y_r.at[w, k], partner
                ).wait_recv()

        total = yrecv[w, 0, y_part(w)].astype(F32)
        for k in range(1, 8):
            total += yrecv[w, k, y_part(w)].astype(F32)
        zsend[w] = total[0:32]
        if w == 0:
            gpart[1] = total[32:40] + total[40:48]

    def over_z(w):
        if w < 3:
            y_sum(w)
        else:
            for step in (1, 2, 3):
                h_copy(step).wait()
            total = htotal[x]
            for step in (1, 2, 3):
                total += hrecv[step - 1].astype(F32)
            zsend[w] = total

        for k in range(2):
            @pl.when(z != 2 * w + k)
            def _():
                z_copy(w, k).start()

            @pl.when(z == 2 * w + k)
            def _():
                zrecv[z] = zsend[w, 16 * k : 16 * k + 16]

    for step in (1, 2, 3):
        e_copy(step).wait()
    over_y(0)
    over_y(1)
    f_over_x()
    over_y(2)
    over_z(0)
    for copy in gain_cols:
        copy.start()
    over_z(3)
    over_z(1)
    over_z(2)

    for k in range(8):
        @pl.when(z != k)
        def _():
            remote(zsend.at[0, 0:16], zrecv.at[k], z_s.at[0, 0], z_r.at[k], partner).wait_recv()

    total = zrecv[0]
    for k in range(1, 8):
        total += zrecv[k]
    fin[tm, 0:16] = total
    for copy in gain_cols:
        copy.wait()
    fin[tm, 16:24] = gpart[1] + grecv[1] + grecv[2] + grecv[3]

    last = []
    for step in range(1, 8):
        last.append(remote(fin.at[tm], fin.at[tm], b_s.at[step - 1], b_r.at[step - 1], b_dev(step)))
        last[-1].start()

    for copy in halo + tile:
        copy.wait_send()
    for k in range(8):
        @pl.when(row != y_row(k))
        def _():
            f_copy(k).wait_send()
            for w in range(3):
                y_copy(w, k).wait_send()

    for w in range(4):
        for k in range(2):
            @pl.when(z != 2 * w + k)
            def _():
                z_copy(w, k).wait_send()

    for copy in last:
        copy.wait()
    scale = 1.0 / math.sqrt(16 * 96 * 128)
    gain_total = fin[0, 16:24]
    for k in range(1, 8):
        gain_total += fin[k, 16:24]
    gain_total *= scale
    gg_out[...] = jnp.concatenate([gain_total[0:1], gain_total[1:2]], axis=1)
    value = fin[:, 0:16].reshape(128, 128) * scale
    wg_out[:, 0:128] = value[0:SHARD]
    wg_out[0:40, 128:C] = value[88:128, 0:64]
    wg_out[40:80, 128:C] = pltpu.roll(value[88:128], 64, 1)[:, 0:64]
    wg_out[80:81, 128:C] = value[81:82, 0:64]


def per_device(features, cotangent, kernel, gain):
    vmem = pl.BlockSpec(memory_space=pltpu.VMEM)
    hbm = pl.BlockSpec(memory_space=pltpu.HBM)
    dma = pltpu.SemaphoreType.DMA
    fg, wg, gg = pl.pallas_call(
        body,
        out_shape=(
            jax.ShapeDtypeStruct((2, ROWS, COLS, C), BF16),
            jax.ShapeDtypeStruct((SHARD, C), F32),
            jax.ShapeDtypeStruct((1, 256), F32),
        ),
        in_specs=[hbm, hbm, hbm, vmem],
        out_specs=(vmem, vmem, vmem),
        scratch_shapes=[
            pltpu.VMEM((2, ROWS, COLS, C), BF16),
            pltpu.VMEM((2, ROWS, COLS, C), BF16),
            pltpu.VMEM((C, 27 * C), BF16),
            pltpu.VMEM((2, 3, 4, ROWS + 2, COLS, C), BF16),
            pltpu.VMEM((2, 2, 2, 3, 16, C), BF16),
            pltpu.VMEM((2, C, CELLS), BF16),
            pltpu.VMEM((2, 16, C), BF16),
            pltpu.VMEM((2, 16, C), F32),
            pltpu.VMEM((CELLS, 256), F32),
            pltpu.VMEM(((LATE + EARLY) * C + 96, 128), F32),
            pltpu.VMEM(((LATE + EARLY) * C + 96, 128), F32),
            pltpu.VMEM((4, 3, 192, 128), BF16),
            pltpu.VMEM((3, 3, 192, 128), BF16),
            pltpu.VMEM((4, 192, 128), BF16),
            pltpu.VMEM((3, 192, 128), BF16),
            pltpu.VMEM((8, 128, 128), BF16),
            pltpu.VMEM((8, 128, 128), BF16),
            pltpu.VMEM((4, 32, 128), F32),
            pltpu.VMEM((4, 32, 128), BF16),
            pltpu.VMEM((3, 32, 128), BF16),
            pltpu.VMEM((2, 8, 128), F32),
            pltpu.VMEM((4, 8, 128), F32),
            pltpu.VMEM((3, 8, 48, 128), BF16),
            pltpu.VMEM((3, 8, 48, 128), BF16),
            pltpu.VMEM((4, 32, 128), F32),
            pltpu.VMEM((8, 16, 128), F32),
            pltpu.VMEM((8, 24, 128), F32),
            dma((3,)),
            dma((len(HALO),)), dma((len(HALO),)), dma((2,)), dma((2,)), dma((8,)), dma((8,)),
            dma((3, 3)), dma((3, 3)), dma((3,)), dma((3,)), dma((8,)), dma((8,)), dma((3,)), dma((3,)), dma((4,)), dma((4,)),
            dma((3, 8)), dma((3, 8)), dma((4, 2)), dma((8,)), dma((7,)), dma((7,)),
        ],
        compiler_params=pltpu.CompilerParams(
            collective_id=0, has_side_effects=True, vmem_limit_bytes=54912 * 1024
        ),
    )(features, cotangent, kernel.T, gain.reshape(1, C))
    return fg, wg, gg[0, :C]


def solution(mesh):
    return jax.shard_map(
        per_device,
        mesh=mesh,
        in_specs=(P("tm", "row", "col", None), P("tm", "row", "col", None), P(), P()),
        out_specs=(P("tm", "row", "col", None), P(("row", "col"), None), P()),
        check_vma=False,
    )
```

```python
import math

import jax
import jax.numpy as jnp
from jax import lax
from jax.experimental import pallas as pl
from jax.experimental.pallas import tpu as pltpu
from jax.sharding import PartitionSpec as P

MESH = pl.DeviceIdType.MESH
F32 = jnp.float32
BF16 = jnp.bfloat16
C = 192
ROWS, COLS = 6, 32
CELLS = 2 * ROWS * COLS
LATE, EARLY = 11, 4
SHARD = 81

HALO = [(0, 1, 0)] + [(0, out, dc) for out in (0, 1) for dc in (-1, 1)]
HALO += [(1, 0, 0), (1, 1, 0)] + [(1, out, dc) for out in (0, 1) for dc in (-1, 1)]
NOW = 5


def body(
    feat_hbm, cot_hbm, w_hbm, gain, fg_out, wg_out, gg_out,
    feat, cot, tsend, trecv, w_v, big, cols, act_t, packs, rows16, act32, wgl_a, wgl_b, xsend, xrecv, esend, erecv, fsend, frecv, htotal, hsend, hrecv,
    gpart, grecv, ysend, yrecv, zsend, zrecv, fin,
    in_sem, halo_s, halo_r, tile_s, tile_r, pair_s, pair_r, x_s, x_r, e_s, e_r, f_s, f_r, h_s, h_r, g_s, g_r, y_s, y_r, z_s, z_r, b_s, b_r,
):
    tm, row, col = lax.axis_index("tm"), lax.axis_index("row"), lax.axis_index("col")
    x, zlo = tm // 2, tm % 2
    y, core = row // 2, row % 2
    z = col * 2 + zlo
    other = 1 - core
    outward = 2 * core - 1
    partner = (tm, 2 * y + other, col)

    def near(dt, dr, dc):
        return ((tm + dt + 8) % 8, (row + dr + 16) % 16, (col + dc + 4) % 4)

    def x_dev(step):
        return (((x + step) % 4) * 2 + zlo, row, col)

    def z_dev(step):
        to = (z + step) % 8
        return (2 * x + to % 2, row, to // 2)

    def b_dev(step):
        return ((tm + step) % 8, row, col)

    def remote(src, dst, send, recv, device):
        return pltpu.make_async_remote_copy(
            src_ref=src, dst_ref=dst, send_sem=send, recv_sem=recv, device_id=device, device_id_type=MESH
        )

    main = big.at[0, 1]
    loads = [
        pltpu.make_async_copy(cot_hbm, cot, in_sem.at[0]),
        pltpu.make_async_copy(feat_hbm, feat, in_sem.at[1]),
        pltpu.make_async_copy(w_hbm, w_v, in_sem.at[2]),
    ]
    for copy in loads:
        copy.start()

    barrier = pltpu.get_barrier_semaphore()

    def greet(device):
        pl.semaphore_signal(barrier, inc=1, device_id=device, device_id_type=MESH)

    for df, out, dc in HALO:
        greet(near(df, outward * out, -dc))
    greet(partner)
    for step in range(1, 4):
        greet(x_dev(4 - step))
    for step in range(1, 8):
        greet(z_dev(8 - step))
        greet(b_dev(8 - step))
    holder = jnp.logical_and(row >= 6, row < 14).astype(jnp.int32)
    self_y = core == holder
    for k in range(8):
        @pl.when(jnp.logical_not(jnp.logical_and(self_y, y == k)))
        def _():
            greet((tm, 2 * k + holder, col))

    loads[0].wait()
    for side, q in ((0, 0), (1, COLS - 1)):
        rows16[side] = jnp.zeros((16, C), F32)
        for f in range(2):
            for r in range(ROWS):
                i = f * ROWS + r
                rows16[side, i : i + 1, :] = cot[f, r].astype(F32)[q : q + 1, :]
        packs[side] = rows16[side].astype(BF16)

    half = CELLS // 2
    act32[:, :C] = cot[...].astype(F32).reshape(CELLS, C)
    side = lax.broadcasted_iota(jnp.int32, (half, 128), 1)
    rest = jnp.where(side < 64, act32[0:half, 128:256], pltpu.roll(act32[half:CELLS, 128:256], 64, 1))
    tsend[0] = cot[0, :, :, 0:128]
    tsend[1] = rest.astype(BF16).reshape(ROWS, COLS, 128)
    tsend[2] = cot[1, :, :, 0:128]

    expected = len(HALO) + 1 + 3 + 7 + 7 + 8
    pl.semaphore_wait(barrier, expected - self_y.astype(jnp.int32))

    halo, tile = [], []
    for m, (df, out, dc) in enumerate(HALO):
        if dc != 0:
            src = packs.at[0 if dc < 0 else 1]
            dst = cols.at[0, df, 1 if dc < 0 else 0, 2 * other if out else 1]
        elif out:
            src, dst = cot.at[:, (ROWS - 1) * core], main.at[2 * df : 2 * df + 2, (ROWS + 1) * other]
        else:
            for n, part in enumerate((slice(0, 2), slice(2, 3))):
                tile.append(remote(
                    tsend.at[part], trecv.at[part], tile_s.at[n], tile_r.at[n], near(-1, 0, 0)
                ))
                tile[-1].start()
            continue
        halo.append(remote(src, dst, halo_s.at[m], halo_r.at[m], near(-df, outward * out, dc)))
        halo[-1].start()

    other_main = big.at[1, 1]
    swap = []

    def hand_over(n, src, dst):
        swap.append(remote(src, dst, pair_s.at[n], pair_r.at[n], partner))
        swap[-1].start()

    hand_over(0, cot, other_main.at[0:2, 1 : ROWS + 1])
    main[0:2, 1 : ROWS + 1] = cot[...]

    def norm():
        wide = feat[...].astype(F32).reshape(CELLS, C)
        inverse = lax.rsqrt(jnp.mean(wide * wide, axis=-1, keepdims=True) + 1e-06)
        normed = wide * inverse
        return inverse, normed, normed * gain[...]

    loads[1].wait()
    pre = norm()[2]
    act32[:, C:] = jnp.zeros((CELLS, 256 - C), F32)
    act32[:, :C] = pre * jax.nn.sigmoid(pre)
    act_t[0] = act32[...].T[:C].astype(BF16)
    hand_over(1, act_t.at[0], act_t.at[1])

    def borders(df):
        f = slice(2 * df, 2 * df + 2)
        if df == 1:
            for n in (0, 1):
                tile[n].wait_recv()
                rest = trecv[1].astype(F32).reshape(CELLS // 2, 128)
                rest = rest if n == 0 else pltpu.roll(rest, 64, 1)
                main[2 + n, 1 : ROWS + 1, :, 0:128] = trecv[2 * n]
                main[2 + n, 1 : ROWS + 1, :, 128:C] = rest[:, 0:64].astype(BF16).reshape(ROWS, COLS, 64)

                @pl.when(tm == 7)
                def _():
                    main[2 + n, 1 : ROWS + 1] = jnp.zeros((ROWS, COLS, C), BF16)

                inner = (2 + n, slice(1, ROWS + 1))
                hand_over(4 + n, main.at[inner], other_main.at[inner])
        for copy in halo[:NOW] if df == 0 else halo[NOW:]:
            copy.wait_recv()

        @pl.when(row == 0)
        def _():
            main[f, 0] = jnp.zeros((2, COLS, C), BF16)
            cols[0, df, :, 0] = jnp.zeros((2, 16, C), BF16)

        @pl.when(row == 15)
        def _():
            main[f, ROWS + 1] = jnp.zeros((2, COLS, C), BF16)
            cols[0, df, :, 2] = jnp.zeros((2, 16, C), BF16)

        if df == 1:
            @pl.when(tm == 7)
            def _():
                main[f, (ROWS + 1) * core] = jnp.zeros((2, COLS, C), BF16)
                cols[0, df] = jnp.zeros((2, 3, 16, C), BF16)

        @pl.when(col == 0)
        def _():
            cols[0, df, 0] = jnp.zeros((3, 16, C), BF16)

        @pl.when(col == 3)
        def _():
            cols[0, df, 1] = jnp.zeros((3, 16, C), BF16)

        edge = (ROWS + 1) * core
        hand_over(2 + 4 * df, main.at[f, edge], other_main.at[f, edge])
        hand_over(3 + 4 * df, cols.at[0, df], cols.at[1, df])
        for copy in swap:
            copy.wait()
        swap.clear()
        main[f, (ROWS + 1) * other] = big[1, 1, f, 1 + (ROWS - 1) * core]
        other_main[f, (ROWS + 1) * core] = main[f, ROWS - (ROWS - 1) * core]
        cols[0, df, :, 2 * other] = cols[1, df, :, 1]
        cols[1, df, :, 2 * core] = cols[0, df, :, 1]

    spot = lax.broadcasted_iota(jnp.int32, (COLS, C), 0)

    def shift(tile, df):
        edges = [[cols[tile, df, s, k].astype(F32) for k in range(3)] for s in (0, 1)]
        for f in (2 * df, 2 * df + 1):
            for r in range(ROWS + 2):
                k = 0 if r == 0 else 2 if r == ROWS + 1 else 1
                i = (f % 2) * ROWS + (r - 1) % ROWS
                value = big[tile, 1, f, r].astype(F32)
                after = jnp.where(spot == COLS - 1, edges[1][k][i : i + 1], pltpu.roll(value, COLS - 1, 0))
                before = jnp.where(spot == 0, edges[0][k][i : i + 1], pltpu.roll(value, 1, 0))
                big[tile, 0, f, r] = after.astype(BF16)
                big[tile, 2, f, r] = before.astype(BF16)

    def tap_grad(tap, at):
        a, b, c = tap // 9, (tap // 3) % 3, tap % 3
        total = jnp.zeros((C, C), F32)
        for tile in (0, 1):
            patch = big[tile, c, pl.ds(2 - a, 2), pl.ds(2 - b, ROWS)].reshape(CELLS, C)
            total += jnp.dot(act_t[tile], patch, preferred_element_type=F32)
        at = pl.multiple_of(at, 8)
        wgl_a[pl.ds(at, C), :] = total[:, 0:128]
        wgl_b[pl.ds(at, C), 0:64] = total[:, 128:C]

    lane = lax.broadcasted_iota(jnp.int32, (40, 128), 1)
    line = lax.broadcasted_iota(jnp.int32, (88, 128), 0)

    def pack(at):
        upper = jnp.where(
            line < SHARD, wgl_a[at : at + 88], jnp.where(line == SHARD, wgl_b[at + 80 : at + 81], 0.0)
        )
        lower = jnp.where(lane < 64, wgl_b[at : at + 40], pltpu.roll(wgl_b[at + 40 : at + 80], 64, 1))
        return jnp.concatenate([upper, lower], axis=0).astype(BF16)

    def e_copy(step):
        return remote(
            esend.at[(x + step) % 4], erecv.at[step - 1], e_s.at[step - 1], e_r.at[step - 1], x_dev(step)
        )

    def y_row(k):
        return k + 6 * core if k < 6 else k + 8 - 2 * core

    def f_copy(k):
        return remote(fsend.at[k], frecv.at[y], f_s.at[k], f_r.at[y], (tm, y_row(k), col))

    def f_start(chunks):
        for k in chunks:
            @pl.when(row != y_row(k))
            def _():
                f_copy(k).start()

            @pl.when(row == y_row(k))
            def _():
                frecv[y] = fsend[k]

    borders(0)
    shift(0, 0)
    shift(1, 0)
    base = LATE * C + 24
    for i in range(EARLY):
        tap_grad(23 - 3 * core + i, base + i * C + 72 * core)
    for j in range(8):
        value = pack(base + 120 + SHARD * j)
        at = 64 * (j % 4) + 32 * (j // 4)
        if j % 4 == 3:
            fsend[6 + j // 4] = value
        else:
            for k in range(4):
                esend[k, at : at + 32] = value[32 * k : 32 * k + 32]
    for step in (1, 2, 3):
        e_copy(step).start()
    f_start((6, 7))

    borders(1)
    shift(0, 1)
    shift(1, 1)
    for i in range(LATE):
        tap_grad(10 * core + i, i * C + 24 * other)
    for j in range(24):
        value = pack(24 + SHARD * j)
        if j % 4 == 3:
            fsend[j // 4] = value
        else:
            for k in range(4):
                xsend[k, j % 4, 32 * (j // 4) : 32 * (j // 4) + 32] = value[32 * k : 32 * k + 32]

    f_start(range(6))

    def h_copy(step):
        return remote(
            hsend.at[(x + step) % 4], hrecv.at[step - 1], h_s.at[step - 1], h_r.at[step - 1], x_dev(step)
        )

    def from_y(k):
        return jnp.logical_not(jnp.logical_and(self_y, y == k))

    def f_over_x():
        for k in range(8):
            @pl.when(from_y(k))
            def _():
                remote(fsend.at[0], frecv.at[k], f_s.at[0], f_r.at[k], partner).wait_recv()

        total = frecv[0].astype(F32)
        for k in range(1, 8):
            total += frecv[k].astype(F32)
        htotal[...] = total.reshape(4, 32, 128)
        hsend[...] = total.astype(BF16).reshape(4, 32, 128)
        for step in (1, 2, 3):
            h_copy(step).start()

    def x_copy(w, step):
        return remote(
            xsend.at[(x + step) % 4, w], xrecv.at[step - 1, w],
            x_s.at[w, step - 1], x_r.at[w, step - 1], x_dev(step),
        )

    def x_start(w):
        for step in (1, 2, 3):
            x_copy(w, step).start()

    x_start(0)
    x_start(1)

    loads[2].wait()
    dact = jnp.zeros((CELLS, C), F32)
    for tap in range(27):
        a, b, c = tap // 9, (tap // 3) % 3, tap % 3
        patch = big[0, c, 2 - a : 4 - a, 2 - b : 2 - b + ROWS].reshape(CELLS, C)
        dact += jnp.dot(patch, w_v[:, tap * C : (tap + 1) * C], preferred_element_type=F32)
    inverse, normed, pre = norm()
    sigma = jax.nn.sigmoid(pre)
    dpre = dact * sigma * (1.0 + pre * (1.0 - sigma))
    gain_part = jnp.sum(dpre * normed, axis=0, keepdims=True)
    dnormed = dpre * gain[...]
    project = jnp.mean(dnormed * normed, axis=-1, keepdims=True)
    grad = cot[...].astype(F32).reshape(CELLS, C) + inverse * (dnormed - normed * project)
    fg_out[...] = grad.astype(BF16).reshape(2, ROWS, COLS, C)

    act32[0:8, :] = jnp.zeros((8, 256), F32)
    act32[0:1, :C] = gain_part
    gpart[0] = act32[0:8, 0:128]
    gpart[0, 1:2] = act32[0:1, 128:256]
    gain_pair = remote(gpart.at[0], grecv.at[0], g_s.at[0], g_r.at[0], partner)
    gain_pair.start()
    gain_cols = [
        remote(gpart.at[1], grecv.at[k], g_s.at[k], g_r.at[k], (tm, row, (col + k) % 4)) for k in (1, 2, 3)
    ]

    def y_part(w):
        return slice(0, 48 if w == 0 else 32)

    def y_copy(w, k):
        return remote(
            ysend.at[w, k, y_part(w)], yrecv.at[w, y, y_part(w)], y_s.at[w, k], y_r.at[w, y],
            (tm, y_row(k), col),
        )

    def z_copy(w, k):
        return remote(
            zsend.at[w, 16 * k : 16 * k + 16], zrecv.at[z], z_s.at[w, k], z_r.at[z], (2 * x + k, row, w)
        )

    def over_y(w):
        part = slice(64 * w, 64 * w + 64)
        extra = esend[x, part].astype(F32)
        for step in (1, 2, 3):
            extra += erecv[step - 1, part].astype(F32)
        ysend[w, 6:8, 0:32] = extra.astype(BF16).reshape(2, 32, 128)
        for step in (1, 2, 3):
            x_copy(w, step).wait()
        if w == 0:
            x_start(2)
        value = xsend[x, w].astype(F32)
        for step in (1, 2, 3):
            value += xrecv[step - 1, w].astype(F32)
        ysend[w, 0:6, 0:32] = value.astype(BF16).reshape(6, 32, 128)
        if w == 0:
            gain_pair.wait()
            total = gpart[0] + grecv[0]
            upper = total.astype(BF16).astype(F32)
            both = jnp.concatenate([upper, total - upper], axis=0).astype(BF16)
            for k in range(8):
                ysend[w, k, 32:48] = both
        for k in range(8):
            @pl.when(row != y_row(k))
            def _():
                y_copy(w, k).start()

            @pl.when(row == y_row(k))
            def _():
                yrecv[w, y, y_part(w)] = ysend[w, k, y_part(w)]

    def y_sum(w):
        for k in range(8):
            @pl.when(from_y(k))
            def _():
                remote(
                    ysend.at[w, 0, y_part(w)], yrecv.at[w, k, y_part(w)], y_s.at[w, 0], y_r.at[w, k], partner
                ).wait_recv()

        total = yrecv[w, 0, y_part(w)].astype(F32)
        for k in range(1, 8):
            total += yrecv[w, k, y_part(w)].astype(F32)
        zsend[w] = total[0:32]
        if w == 0:
            gpart[1] = total[32:40] + total[40:48]

    def over_z(w):
        if w < 3:
            y_sum(w)
        else:
            for step in (1, 2, 3):
                h_copy(step).wait()
            total = htotal[x]
            for step in (1, 2, 3):
                total += hrecv[step - 1].astype(F32)
            zsend[w] = total

        for k in range(2):
            @pl.when(z != 2 * w + k)
            def _():
                z_copy(w, k).start()

            @pl.when(z == 2 * w + k)
            def _():
                zrecv[z] = zsend[w, 16 * k : 16 * k + 16]

    for step in (1, 2, 3):
        e_copy(step).wait()
    over_y(0)
    over_y(1)
    f_over_x()
    over_y(2)
    over_z(0)
    for copy in gain_cols:
        copy.start()
    over_z(3)
    over_z(1)
    over_z(2)

    for k in range(8):
        @pl.when(z != k)
        def _():
            remote(zsend.at[0, 0:16], zrecv.at[k], z_s.at[0, 0], z_r.at[k], partner).wait_recv()

    total = zrecv[0]
    for k in range(1, 8):
        total += zrecv[k]
    fin[tm, 0:16] = total
    for copy in gain_cols:
        copy.wait()
    fin[tm, 16:24] = gpart[1] + grecv[1] + grecv[2] + grecv[3]

    last = []
    for step in range(1, 8):
        last.append(remote(fin.at[tm], fin.at[tm], b_s.at[step - 1], b_r.at[step - 1], b_dev(step)))
        last[-1].start()

    for copy in halo + tile:
        copy.wait_send()
    for k in range(8):
        @pl.when(row != y_row(k))
        def _():
            f_copy(k).wait_send()
            for w in range(3):
                y_copy(w, k).wait_send()

    for w in range(4):
        for k in range(2):
            @pl.when(z != 2 * w + k)
            def _():
                z_copy(w, k).wait_send()

    for copy in last:
        copy.wait()
    scale = 1.0 / math.sqrt(16 * 96 * 128)
    gain_total = fin[0, 16:24]
    for k in range(1, 8):
        gain_total += fin[k, 16:24]
    gain_total *= scale
    gg_out[...] = jnp.concatenate([gain_total[0:1], gain_total[1:2]], axis=1)
    value = fin[:, 0:16].reshape(128, 128) * scale
    wg_out[:, 0:128] = value[0:SHARD]
    wg_out[0:40, 128:C] = value[88:128, 0:64]
    wg_out[40:80, 128:C] = pltpu.roll(value[88:128], 64, 1)[:, 0:64]
    wg_out[80:81, 128:C] = value[81:82, 0:64]


def per_device(features, cotangent, kernel, gain):
    vmem = pl.BlockSpec(memory_space=pltpu.VMEM)
    hbm = pl.BlockSpec(memory_space=pltpu.HBM)
    dma = pltpu.SemaphoreType.DMA
    fg, wg, gg = pl.pallas_call(
        body,
        out_shape=(
            jax.ShapeDtypeStruct((2, ROWS, COLS, C), BF16),
            jax.ShapeDtypeStruct((SHARD, C), F32),
            jax.ShapeDtypeStruct((1, 256), F32),
        ),
        in_specs=[hbm, hbm, hbm, vmem],
        out_specs=(vmem, vmem, vmem),
        scratch_shapes=[
            pltpu.VMEM((2, ROWS, COLS, C), BF16),
            pltpu.VMEM((2, ROWS, COLS, C), BF16),
            pltpu.VMEM((3, ROWS, COLS, 128), BF16),
            pltpu.VMEM((3, ROWS, COLS, 128), BF16),
            pltpu.VMEM((C, 27 * C), BF16),
            pltpu.VMEM((2, 3, 4, ROWS + 2, COLS, C), BF16),
            pltpu.VMEM((2, 2, 2, 3, 16, C), BF16),
            pltpu.VMEM((2, C, CELLS), BF16),
            pltpu.VMEM((2, 16, C), BF16),
            pltpu.VMEM((2, 16, C), F32),
            pltpu.VMEM((CELLS, 256), F32),
            pltpu.VMEM(((LATE + EARLY) * C + 96, 128), F32),
            pltpu.VMEM(((LATE + EARLY) * C + 96, 128), F32),
            pltpu.VMEM((4, 3, 192, 128), BF16),
            pltpu.VMEM((3, 3, 192, 128), BF16),
            pltpu.VMEM((4, 192, 128), BF16),
            pltpu.VMEM((3, 192, 128), BF16),
            pltpu.VMEM((8, 128, 128), BF16),
            pltpu.VMEM((8, 128, 128), BF16),
            pltpu.VMEM((4, 32, 128), F32),
            pltpu.VMEM((4, 32, 128), BF16),
            pltpu.VMEM((3, 32, 128), BF16),
            pltpu.VMEM((2, 8, 128), F32),
            pltpu.VMEM((4, 8, 128), F32),
            pltpu.VMEM((3, 8, 48, 128), BF16),
            pltpu.VMEM((3, 8, 48, 128), BF16),
            pltpu.VMEM((4, 32, 128), F32),
            pltpu.VMEM((8, 16, 128), F32),
            pltpu.VMEM((8, 24, 128), F32),
            dma((3,)),
            dma((len(HALO),)), dma((len(HALO),)), dma((2,)), dma((2,)), dma((8,)), dma((8,)),
            dma((3, 3)), dma((3, 3)), dma((3,)), dma((3,)), dma((8,)), dma((8,)), dma((3,)), dma((3,)), dma((4,)), dma((4,)),
            dma((3, 8)), dma((3, 8)), dma((4, 2)), dma((8,)), dma((7,)), dma((7,)),
        ],
        compiler_params=pltpu.CompilerParams(
            collective_id=0, has_side_effects=True, vmem_limit_bytes=54912 * 1024
        ),
    )(features, cotangent, kernel.T, gain.reshape(1, C))
    return fg, wg, gg[0, :C]


def solution(mesh):
    return jax.shard_map(
        per_device,
        mesh=mesh,
        in_specs=(P("tm", "row", "col", None), P("tm", "row", "col", None), P(), P()),
        out_specs=(P("tm", "row", "col", None), P(("row", "col"), None), P()),
        check_vma=False,
    )
```

```python
import math

import jax
import jax.numpy as jnp
from jax import lax
from jax.experimental import pallas as pl
from jax.experimental.pallas import tpu as pltpu
from jax.sharding import PartitionSpec as P

MESH = pl.DeviceIdType.MESH
F32 = jnp.float32
BF16 = jnp.bfloat16
C = 192
ROWS, COLS = 6, 32
CELLS = 2 * ROWS * COLS
LATE, EARLY = 11, 4
SHARD = 81

HALO = [(0, 1, 0)] + [(0, out, dc) for out in (0, 1) for dc in (-1, 1)]
HALO += [(1, out, dc) for out in (0, 1) for dc in (-1, 1)] + [(1, 1, 0), (1, 0, 0)]
NOW = 5


def body(
    feat_hbm, cot_hbm, w_hbm, gain, fg_out, wg_out, gg_out,
    feat, cot, tsend, trecv, w_v, big, cols, act_t, packs, rows16, act32, wgl_a, wgl_b, xsend, xrecv, esend, erecv, fsend, frecv, htotal, hsend, hrecv,
    gpart, grecv, ysend, yrecv, zsend, zrecv, fin,
    in_sem, halo_s, halo_r, tile_s, tile_r, pair_s, pair_r, x_s, x_r, e_s, e_r, f_s, f_r, h_s, h_r, g_s, g_r, y_s, y_r, z_s, z_r, b_s, b_r,
):
    tm, row, col = lax.axis_index("tm"), lax.axis_index("row"), lax.axis_index("col")
    x, zlo = tm // 2, tm % 2
    y, core = row // 2, row % 2
    z = col * 2 + zlo
    other = 1 - core
    outward = 2 * core - 1
    partner = (tm, 2 * y + other, col)

    def near(dt, dr, dc):
        return ((tm + dt + 8) % 8, (row + dr + 16) % 16, (col + dc + 4) % 4)

    def x_dev(step):
        return (((x + step) % 4) * 2 + zlo, row, col)

    def z_dev(step):
        to = (z + step) % 8
        return (2 * x + to % 2, row, to // 2)

    def b_dev(step):
        return ((tm + step) % 8, row, col)

    def remote(src, dst, send, recv, device):
        return pltpu.make_async_remote_copy(
            src_ref=src, dst_ref=dst, send_sem=send, recv_sem=recv, device_id=device, device_id_type=MESH
        )

    main = big.at[0, 1]
    loads = [
        pltpu.make_async_copy(cot_hbm, cot, in_sem.at[0]),
        pltpu.make_async_copy(feat_hbm, feat, in_sem.at[1]),
        pltpu.make_async_copy(w_hbm, w_v, in_sem.at[2]),
    ]
    for copy in loads:
        copy.start()

    barrier = pltpu.get_barrier_semaphore()

    def greet(device):
        pl.semaphore_signal(barrier, inc=1, device_id=device, device_id_type=MESH)

    for df, out, dc in HALO:
        greet(near(df, outward * out, -dc))
    greet(partner)
    for step in range(1, 4):
        greet(x_dev(4 - step))
    for step in range(1, 8):
        greet(z_dev(8 - step))
        greet(b_dev(8 - step))
    holder = jnp.logical_and(row >= 6, row < 14).astype(jnp.int32)
    self_y = core == holder
    for k in range(8):
        @pl.when(jnp.logical_not(jnp.logical_and(self_y, y == k)))
        def _():
            greet((tm, 2 * k + holder, col))

    loads[0].wait()
    for side, q in ((0, 0), (1, COLS - 1)):
        rows16[side] = jnp.zeros((16, C), F32)
        for f in range(2):
            for r in range(ROWS):
                i = f * ROWS + r
                rows16[side, i : i + 1, :] = cot[f, r].astype(F32)[q : q + 1, :]
        packs[side] = rows16[side].astype(BF16)

    half = CELLS // 2
    act32[:, :C] = cot[...].astype(F32).reshape(CELLS, C)
    side = lax.broadcasted_iota(jnp.int32, (half, 128), 1)
    rest = jnp.where(side < 64, act32[0:half, 128:256], pltpu.roll(act32[half:CELLS, 128:256], 64, 1))
    tsend[0] = cot[0, :, :, 0:128]
    tsend[1] = rest.astype(BF16).reshape(ROWS, COLS, 128)
    tsend[2] = cot[1, :, :, 0:128]

    expected = len(HALO) + 1 + 3 + 7 + 7 + 8
    pl.semaphore_wait(barrier, expected - self_y.astype(jnp.int32))

    halo, tile = [], []
    for m, (df, out, dc) in enumerate(HALO):
        if dc != 0:
            src = packs.at[0 if dc < 0 else 1]
            dst = cols.at[0, df, 1 if dc < 0 else 0, 2 * other if out else 1]
        elif out:
            src, dst = cot.at[:, (ROWS - 1) * core], main.at[2 * df : 2 * df + 2, (ROWS + 1) * other]
        else:
            for n, part in enumerate((slice(0, 2), slice(2, 3))):
                tile.append(remote(
                    tsend.at[part], trecv.at[part], tile_s.at[n], tile_r.at[n], near(-1, 0, 0)
                ))
                tile[-1].start()
            continue
        halo.append(remote(src, dst, halo_s.at[m], halo_r.at[m], near(-df, outward * out, dc)))
        halo[-1].start()

    other_main = big.at[1, 1]
    swap = []

    def hand_over(n, src, dst):
        swap.append(remote(src, dst, pair_s.at[n], pair_r.at[n], partner))
        swap[-1].start()

    hand_over(0, cot, other_main.at[0:2, 1 : ROWS + 1])
    main[0:2, 1 : ROWS + 1] = cot[...]

    def norm():
        wide = feat[...].astype(F32).reshape(CELLS, C)
        inverse = lax.rsqrt(jnp.mean(wide * wide, axis=-1, keepdims=True) + 1e-06)
        normed = wide * inverse
        return inverse, normed, normed * gain[...]

    loads[1].wait()
    pre = norm()[2]
    act32[:, C:] = jnp.zeros((CELLS, 256 - C), F32)
    act32[:, :C] = pre * jax.nn.sigmoid(pre)
    act_t[0] = act32[...].T[:C].astype(BF16)
    hand_over(1, act_t.at[0], act_t.at[1])

    def borders(df):
        f = slice(2 * df, 2 * df + 2)
        if df == 1:
            for n in (0, 1):
                tile[n].wait_recv()
                rest = trecv[1].astype(F32).reshape(CELLS // 2, 128)
                rest = rest if n == 0 else pltpu.roll(rest, 64, 1)
                main[2 + n, 1 : ROWS + 1, :, 0:128] = trecv[2 * n]
                main[2 + n, 1 : ROWS + 1, :, 128:C] = rest[:, 0:64].astype(BF16).reshape(ROWS, COLS, 64)

                @pl.when(tm == 7)
                def _():
                    main[2 + n, 1 : ROWS + 1] = jnp.zeros((ROWS, COLS, C), BF16)

                inner = (2 + n, slice(1, ROWS + 1))
                hand_over(4 + n, main.at[inner], other_main.at[inner])
        for copy in halo[:NOW] if df == 0 else halo[NOW:]:
            copy.wait_recv()

        @pl.when(row == 0)
        def _():
            main[f, 0] = jnp.zeros((2, COLS, C), BF16)
            cols[0, df, :, 0] = jnp.zeros((2, 16, C), BF16)

        @pl.when(row == 15)
        def _():
            main[f, ROWS + 1] = jnp.zeros((2, COLS, C), BF16)
            cols[0, df, :, 2] = jnp.zeros((2, 16, C), BF16)

        if df == 1:
            @pl.when(tm == 7)
            def _():
                main[f, (ROWS + 1) * core] = jnp.zeros((2, COLS, C), BF16)
                cols[0, df] = jnp.zeros((2, 3, 16, C), BF16)

        @pl.when(col == 0)
        def _():
            cols[0, df, 0] = jnp.zeros((3, 16, C), BF16)

        @pl.when(col == 3)
        def _():
            cols[0, df, 1] = jnp.zeros((3, 16, C), BF16)

        edge = (ROWS + 1) * core
        hand_over(2 + 4 * df, main.at[f, edge], other_main.at[f, edge])
        hand_over(3 + 4 * df, cols.at[0, df], cols.at[1, df])
        for copy in swap:
            copy.wait()
        swap.clear()
        main[f, (ROWS + 1) * other] = big[1, 1, f, 1 + (ROWS - 1) * core]
        other_main[f, (ROWS + 1) * core] = main[f, ROWS - (ROWS - 1) * core]
        cols[0, df, :, 2 * other] = cols[1, df, :, 1]
        cols[1, df, :, 2 * core] = cols[0, df, :, 1]

    spot = lax.broadcasted_iota(jnp.int32, (COLS, C), 0)

    def shift(tile, df):
        edges = [[cols[tile, df, s, k].astype(F32) for k in range(3)] for s in (0, 1)]
        for f in (2 * df, 2 * df + 1):
            for r in range(ROWS + 2):
                k = 0 if r == 0 else 2 if r == ROWS + 1 else 1
                i = (f % 2) * ROWS + (r - 1) % ROWS
                value = big[tile, 1, f, r].astype(F32)
                after = jnp.where(spot == COLS - 1, edges[1][k][i : i + 1], pltpu.roll(value, COLS - 1, 0))
                before = jnp.where(spot == 0, edges[0][k][i : i + 1], pltpu.roll(value, 1, 0))
                big[tile, 0, f, r] = after.astype(BF16)
                big[tile, 2, f, r] = before.astype(BF16)

    def tap_grad(tap, at):
        a, b, c = tap // 9, (tap // 3) % 3, tap % 3
        total = jnp.zeros((C, C), F32)
        for tile in (0, 1):
            patch = big[tile, c, pl.ds(2 - a, 2), pl.ds(2 - b, ROWS)].reshape(CELLS, C)
            total += jnp.dot(act_t[tile], patch, preferred_element_type=F32)
        at = pl.multiple_of(at, 8)
        wgl_a[pl.ds(at, C), :] = total[:, 0:128]
        wgl_b[pl.ds(at, C), 0:64] = total[:, 128:C]

    lane = lax.broadcasted_iota(jnp.int32, (40, 128), 1)
    line = lax.broadcasted_iota(jnp.int32, (88, 128), 0)

    def pack(at):
        upper = jnp.where(
            line < SHARD, wgl_a[at : at + 88], jnp.where(line == SHARD, wgl_b[at + 80 : at + 81], 0.0)
        )
        lower = jnp.where(lane < 64, wgl_b[at : at + 40], pltpu.roll(wgl_b[at + 40 : at + 80], 64, 1))
        return jnp.concatenate([upper, lower], axis=0).astype(BF16)

    def e_copy(step):
        return remote(
            esend.at[(x + step) % 4], erecv.at[step - 1], e_s.at[step - 1], e_r.at[step - 1], x_dev(step)
        )

    def y_row(k):
        return k + 6 * core if k < 6 else k + 8 - 2 * core

    def f_copy(k):
        return remote(fsend.at[k], frecv.at[y], f_s.at[k], f_r.at[y], (tm, y_row(k), col))

    def f_start(chunks):
        for k in chunks:
            @pl.when(row != y_row(k))
            def _():
                f_copy(k).start()

            @pl.when(row == y_row(k))
            def _():
                frecv[y] = fsend[k]

    borders(0)
    shift(0, 0)
    shift(1, 0)
    base = LATE * C + 24
    for i in range(EARLY):
        tap_grad(23 - 3 * core + i, base + i * C + 72 * core)
    for j in range(8):
        value = pack(base + 120 + SHARD * j)
        at = 64 * (j % 4) + 32 * (j // 4)
        if j % 4 == 3:
            fsend[6 + j // 4] = value
        else:
            for k in range(4):
                esend[k, at : at + 32] = value[32 * k : 32 * k + 32]
    for step in (1, 2, 3):
        e_copy(step).start()
    f_start((6, 7))

    borders(1)
    shift(0, 1)
    shift(1, 1)
    for i in range(LATE):
        tap_grad(10 * core + i, i * C + 24 * other)
    for j in range(24):
        value = pack(24 + SHARD * j)
        if j % 4 == 3:
            fsend[j // 4] = value
        else:
            for k in range(4):
                xsend[k, j % 4, 32 * (j // 4) : 32 * (j // 4) + 32] = value[32 * k : 32 * k + 32]

    f_start(range(6))

    def h_copy(step):
        return remote(
            hsend.at[(x + step) % 4], hrecv.at[step - 1], h_s.at[step - 1], h_r.at[step - 1], x_dev(step)
        )

    def from_y(k):
        return jnp.logical_not(jnp.logical_and(self_y, y == k))

    def f_over_x():
        for k in range(8):
            @pl.when(from_y(k))
            def _():
                remote(fsend.at[0], frecv.at[k], f_s.at[0], f_r.at[k], partner).wait_recv()

        total = frecv[0].astype(F32)
        for k in range(1, 8):
            total += frecv[k].astype(F32)
        htotal[...] = total.reshape(4, 32, 128)
        hsend[...] = total.astype(BF16).reshape(4, 32, 128)
        for step in (1, 2, 3):
            h_copy(step).start()

    def x_copy(w, step):
        return remote(
            xsend.at[(x + step) % 4, w], xrecv.at[step - 1, w],
            x_s.at[w, step - 1], x_r.at[w, step - 1], x_dev(step),
        )

    def x_start(w):
        for step in (1, 2, 3):
            x_copy(w, step).start()

    x_start(0)
    x_start(1)

    loads[2].wait()
    dact = jnp.zeros((CELLS, C), F32)
    for tap in range(27):
        a, b, c = tap // 9, (tap // 3) % 3, tap % 3
        patch = big[0, c, 2 - a : 4 - a, 2 - b : 2 - b + ROWS].reshape(CELLS, C)
        dact += jnp.dot(patch, w_v[:, tap * C : (tap + 1) * C], preferred_element_type=F32)
    inverse, normed, pre = norm()
    sigma = jax.nn.sigmoid(pre)
    dpre = dact * sigma * (1.0 + pre * (1.0 - sigma))
    gain_part = jnp.sum(dpre * normed, axis=0, keepdims=True)
    dnormed = dpre * gain[...]
    project = jnp.mean(dnormed * normed, axis=-1, keepdims=True)
    grad = cot[...].astype(F32).reshape(CELLS, C) + inverse * (dnormed - normed * project)
    fg_out[...] = grad.astype(BF16).reshape(2, ROWS, COLS, C)

    act32[0:8, :] = jnp.zeros((8, 256), F32)
    act32[0:1, :C] = gain_part
    gpart[0] = act32[0:8, 0:128]
    gpart[0, 1:2] = act32[0:1, 128:256]
    gain_pair = remote(gpart.at[0], grecv.at[0], g_s.at[0], g_r.at[0], partner)
    gain_pair.start()
    gain_cols = [
        remote(gpart.at[1], grecv.at[k], g_s.at[k], g_r.at[k], (tm, row, (col + k) % 4)) for k in (1, 2, 3)
    ]

    def y_part(w):
        return slice(0, 48 if w == 0 else 32)

    def y_copy(w, k):
        return remote(
            ysend.at[w, k, y_part(w)], yrecv.at[w, y, y_part(w)], y_s.at[w, k], y_r.at[w, y],
            (tm, y_row(k), col),
        )

    def z_copy(w, k):
        return remote(
            zsend.at[w, 16 * k : 16 * k + 16], zrecv.at[z], z_s.at[w, k], z_r.at[z], (2 * x + k, row, w)
        )

    def over_y(w):
        part = slice(64 * w, 64 * w + 64)
        extra = esend[x, part].astype(F32)
        for step in (1, 2, 3):
            extra += erecv[step - 1, part].astype(F32)
        ysend[w, 6:8, 0:32] = extra.astype(BF16).reshape(2, 32, 128)
        for step in (1, 2, 3):
            x_copy(w, step).wait()
        if w == 0:
            x_start(2)
        value = xsend[x, w].astype(F32)
        for step in (1, 2, 3):
            value += xrecv[step - 1, w].astype(F32)
        ysend[w, 0:6, 0:32] = value.astype(BF16).reshape(6, 32, 128)
        if w == 0:
            gain_pair.wait()
            total = gpart[0] + grecv[0]
            upper = total.astype(BF16).astype(F32)
            both = jnp.concatenate([upper, total - upper], axis=0).astype(BF16)
            for k in range(8):
                ysend[w, k, 32:48] = both
        for k in range(8):
            @pl.when(row != y_row(k))
            def _():
                y_copy(w, k).start()

            @pl.when(row == y_row(k))
            def _():
                yrecv[w, y, y_part(w)] = ysend[w, k, y_part(w)]

    def y_sum(w):
        for k in range(8):
            @pl.when(from_y(k))
            def _():
                remote(
                    ysend.at[w, 0, y_part(w)], yrecv.at[w, k, y_part(w)], y_s.at[w, 0], y_r.at[w, k], partner
                ).wait_recv()

        total = yrecv[w, 0, y_part(w)].astype(F32)
        for k in range(1, 8):
            total += yrecv[w, k, y_part(w)].astype(F32)
        zsend[w] = total[0:32]
        if w == 0:
            gpart[1] = total[32:40] + total[40:48]

    def over_z(w):
        if w < 3:
            y_sum(w)
        else:
            for step in (1, 2, 3):
                h_copy(step).wait()
            total = htotal[x]
            for step in (1, 2, 3):
                total += hrecv[step - 1].astype(F32)
            zsend[w] = total

        for k in range(2):
            @pl.when(z != 2 * w + k)
            def _():
                z_copy(w, k).start()

            @pl.when(z == 2 * w + k)
            def _():
                zrecv[z] = zsend[w, 16 * k : 16 * k + 16]

    for step in (1, 2, 3):
        e_copy(step).wait()
    over_y(0)
    over_y(1)
    f_over_x()
    over_y(2)
    over_z(0)
    for copy in gain_cols:
        copy.start()
    over_z(3)
    over_z(1)
    over_z(2)

    for k in range(8):
        @pl.when(z != k)
        def _():
            remote(zsend.at[0, 0:16], zrecv.at[k], z_s.at[0, 0], z_r.at[k], partner).wait_recv()

    total = zrecv[0]
    for k in range(1, 8):
        total += zrecv[k]
    fin[tm, 0:16] = total
    for copy in gain_cols:
        copy.wait()
    fin[tm, 16:24] = gpart[1] + grecv[1] + grecv[2] + grecv[3]

    last = []
    for step in range(1, 8):
        last.append(remote(fin.at[tm], fin.at[tm], b_s.at[step - 1], b_r.at[step - 1], b_dev(step)))
        last[-1].start()

    for copy in halo + tile:
        copy.wait_send()
    for k in range(8):
        @pl.when(row != y_row(k))
        def _():
            f_copy(k).wait_send()
            for w in range(3):
                y_copy(w, k).wait_send()

    for w in range(4):
        for k in range(2):
            @pl.when(z != 2 * w + k)
            def _():
                z_copy(w, k).wait_send()

    for copy in last:
        copy.wait()
    scale = 1.0 / math.sqrt(16 * 96 * 128)
    gain_total = fin[0, 16:24]
    for k in range(1, 8):
        gain_total += fin[k, 16:24]
    gain_total *= scale
    gg_out[...] = jnp.concatenate([gain_total[0:1], gain_total[1:2]], axis=1)
    value = fin[:, 0:16].reshape(128, 128) * scale
    wg_out[:, 0:128] = value[0:SHARD]
    wg_out[0:40, 128:C] = value[88:128, 0:64]
    wg_out[40:80, 128:C] = pltpu.roll(value[88:128], 64, 1)[:, 0:64]
    wg_out[80:81, 128:C] = value[81:82, 0:64]


def per_device(features, cotangent, kernel, gain):
    vmem = pl.BlockSpec(memory_space=pltpu.VMEM)
    hbm = pl.BlockSpec(memory_space=pltpu.HBM)
    dma = pltpu.SemaphoreType.DMA
    fg, wg, gg = pl.pallas_call(
        body,
        out_shape=(
            jax.ShapeDtypeStruct((2, ROWS, COLS, C), BF16),
            jax.ShapeDtypeStruct((SHARD, C), F32),
            jax.ShapeDtypeStruct((1, 256), F32),
        ),
        in_specs=[hbm, hbm, hbm, vmem],
        out_specs=(vmem, vmem, vmem),
        scratch_shapes=[
            pltpu.VMEM((2, ROWS, COLS, C), BF16),
            pltpu.VMEM((2, ROWS, COLS, C), BF16),
            pltpu.VMEM((3, ROWS, COLS, 128), BF16),
            pltpu.VMEM((3, ROWS, COLS, 128), BF16),
            pltpu.VMEM((C, 27 * C), BF16),
            pltpu.VMEM((2, 3, 4, ROWS + 2, COLS, C), BF16),
            pltpu.VMEM((2, 2, 2, 3, 16, C), BF16),
            pltpu.VMEM((2, C, CELLS), BF16),
            pltpu.VMEM((2, 16, C), BF16),
            pltpu.VMEM((2, 16, C), F32),
            pltpu.VMEM((CELLS, 256), F32),
            pltpu.VMEM(((LATE + EARLY) * C + 96, 128), F32),
            pltpu.VMEM(((LATE + EARLY) * C + 96, 128), F32),
            pltpu.VMEM((4, 3, 192, 128), BF16),
            pltpu.VMEM((3, 3, 192, 128), BF16),
            pltpu.VMEM((4, 192, 128), BF16),
            pltpu.VMEM((3, 192, 128), BF16),
            pltpu.VMEM((8, 128, 128), BF16),
            pltpu.VMEM((8, 128, 128), BF16),
            pltpu.VMEM((4, 32, 128), F32),
            pltpu.VMEM((4, 32, 128), BF16),
            pltpu.VMEM((3, 32, 128), BF16),
            pltpu.VMEM((2, 8, 128), F32),
            pltpu.VMEM((4, 8, 128), F32),
            pltpu.VMEM((3, 8, 48, 128), BF16),
            pltpu.VMEM((3, 8, 48, 128), BF16),
            pltpu.VMEM((4, 32, 128), F32),
            pltpu.VMEM((8, 16, 128), F32),
            pltpu.VMEM((8, 24, 128), F32),
            dma((3,)),
            dma((len(HALO),)), dma((len(HALO),)), dma((2,)), dma((2,)), dma((8,)), dma((8,)),
            dma((3, 3)), dma((3, 3)), dma((3,)), dma((3,)), dma((8,)), dma((8,)), dma((3,)), dma((3,)), dma((4,)), dma((4,)),
            dma((3, 8)), dma((3, 8)), dma((4, 2)), dma((8,)), dma((7,)), dma((7,)),
        ],
        compiler_params=pltpu.CompilerParams(
            collective_id=0, has_side_effects=True, vmem_limit_bytes=54912 * 1024
        ),
    )(features, cotangent, kernel.T, gain.reshape(1, C))
    return fg, wg, gg[0, :C]


def solution(mesh):
    return jax.shard_map(
        per_device,
        mesh=mesh,
        in_specs=(P("tm", "row", "col", None), P("tm", "row", "col", None), P(), P()),
        out_specs=(P("tm", "row", "col", None), P(("row", "col"), None), P()),
        check_vma=False,
    )
```
